32 devices in a mesh: groups: 2 (over x), seq: 8 (over z, y), wide: 2 (over core).
Axes of the slice: x: 2, y: 2, z: 4, core: 2. Of those that a mesh axis runs over, the one named last changes fastest.
Arguments:
- fine_input: bfloat16 [2, 1536, 768], P('groups', 'seq', 'wide'), parts along dimension 0, may hold values from -6 to 6
- conv_weight: bfloat16 [5, 768, 1536], P(None, 'wide'), may hold values from -0.09375 to 0.09375
- conv_bias: float32 [1536], replicated, may hold values from -3 to 3
- norm_gain: float32 [1536], replicated, may hold values from 0.25 to 1.75
- query_weight: bfloat16 [1536, 768], P(None, 'wide'), may hold values from -0.15625 to 0.15625
- key_weight: bfloat16 [1536, 768], P(None, 'wide'), may hold values from -0.15625 to 0.15625
- value_weight: bfloat16 [1536, 768], P(None, 'wide'), may hold values from -0.15625 to 0.15625
- out_weight: bfloat16 [768, 1536], P('wide'), may hold values from -0.21875 to 0.21875
- cotangent: bfloat16 [2, 768, 1536], P('groups', 'seq'), parts along dimension 0, may hold values from -6 to 6
Outputs:
- section_out: bfloat16 [2, 768, 1536], P('groups', 'seq'), parts along dimension 0
- input_grad: bfloat16 [2, 1536, 768], P('groups', 'seq', 'wide'), parts along dimension 0
- value_grad: float32 [1536, 1536], P(('groups', 'wide'), 'seq'), parts along dimension 0
The draws below stay inside these ranges and needn't reach their ends.
There are 2 independent parts, one for each index of `groups`. The reference program is written for one: setup_inputs(seed, part) draws one part's arguments, and reference() takes and returns one part's arrays. A program takes and returns all parts, laid end to end along the dimension named above; an argument that names none is the same for every part. Nothing has to cross between parts.
All inputs are finite; a program needn't handle non-finite values.
Results may differ from the reference program's by a relative error of at most 0.02.
Values may be sent and summed in bfloat16 or wider, within the bound.
No kernel may reach another device: no remote copies, remote signals or barrier semaphores. Data moves between devices by JAX's collectives and lax.ppermute only.
A program may use at most 128 MiB of HBM per device.

```python
import math
import jax
import jax.numpy as jnp
from jax import lax

SAMPLES = 1
CIN = 768
D = 1536
DH = 192
KW = 5
HD = 768
TOKENS = 768
FINE = 1536


def spiked(array, rng, source, target, parts, factor):
    owner, partner = [(jnp.arange(array.shape[position]) // (array.shape[position] // parts)).reshape([-1 if axis == position else 1 for axis in range(array.ndim)]) for position in (source, target)]
    chosen = jax.random.permutation(rng, parts)[partner]
    strong = (owner == chosen) | (owner == (partner + parts // 2) % parts)
    return jnp.where(strong, factor * array, array)


def block_levels(own_key, dims, pieces, least, high):
    factor_of, own = 1.0, jax.random.fold_in(own_key, 6)
    for dim, blocks in pieces:
        heights = jnp.exp(jax.random.uniform(jax.random.fold_in(own, dim), (blocks,), jnp.float32, least / len(pieces), high / len(pieces)))
        factor_of = factor_of * jnp.repeat(heights, dims[dim] // blocks).reshape([-1 if axis == dim else 1 for axis in range(len(dims))])
    return factor_of


def normal_values(key, extent, spread, limit, cuts=(), kind=jnp.bfloat16):
    array = jax.random.normal(key, extent, jnp.float32) * spread
    if len(cuts) > 0:
        array = block_levels(key, extent, cuts, -0.22, 0.18) * array
    return jnp.clip(array, min=-limit, max=limit).astype(kind)


def noise_with(rng, extent, scale, most, pieces, heavy, held_as=jnp.bfloat16):
    values = scale * jax.random.normal(rng, extent, jnp.float32)
    if pieces:
        values = values * block_levels(rng, extent, pieces, -0.22, 0.18)
    return jnp.clip(spiked(values, jax.random.fold_in(rng, 3), *heavy), -most, most).astype(held_as)


def setup_inputs(seed: int = 0, part: int = 0) -> dict:
    splits = jax.random.split(jax.random.key(seed), 10)
    own_keys = jax.random.split(jax.random.fold_in(splits[9], part), 10)
    return {
        "fine_input": normal_values(own_keys[0], (SAMPLES, FINE, CIN), 1.0, 6.0, ((1, 8), (2, 2))),
        "conv_weight": normal_values(splits[1], (KW, CIN, D), (KW * CIN) ** -0.5, 0.09375, ((1, 2),)),
        "conv_bias": normal_values(splits[2], (D,), 0.5, 3.0, (), jnp.float32),
        "norm_gain": jnp.clip(1.0 + 0.15 * jax.random.normal(splits[3], (D,), jnp.float32), 0.25, 1.75),
        "query_weight": normal_values(splits[4], (D, HD), D ** -0.5, 0.15625, ((1, 2),)),
        "key_weight": normal_values(splits[5], (D, HD), D ** -0.5, 0.15625, ((1, 2),)),
        "value_weight": normal_values(splits[6], (D, HD), D ** -0.5, 0.15625, ((1, 2),)),
        "out_weight": normal_values(splits[7], (HD, D), HD ** -0.5, 0.21875, ((0, 2),)),
        "cotangent": noise_with(own_keys[8], (SAMPLES, TOKENS, D), 1.0, 6.0, ((1, 8),), (1, 2, 8, 2.0)),
    }


EPSILON = 1e-06
SCORE_GAIN = 3.0
GELU_ROOT = 0.7978845608028654
GELU_CUBIC = 0.044715

def gelu_parts(preact):
    tangent = jnp.tanh(GELU_ROOT * (preact + GELU_CUBIC * preact * preact * preact))
    gelu_value = 0.5 * preact * (1.0 + tangent)
    gelu_slope = 0.5 * (1.0 + tangent) + 0.5 * preact * (1.0 - tangent * tangent) * GELU_ROOT * (1.0 + 3.0 * GELU_CUBIC * preact * preact)
    return (gelu_value, gelu_slope)

def matmul(left_op, right_op):
    flat = left_op.reshape(-1, left_op.shape[-1])
    result = jnp.dot(flat, right_op, preferred_element_type=jnp.float32)
    return result.reshape(left_op.shape[:-1] + (right_op.shape[-1],))

def matmul_t(left_op, right_op):
    return matmul(left_op, right_op.T)

def head_norm(projected):
    head_split = projected.reshape(projected.shape[:-1] + (projected.shape[-1] // DH, DH))
    inverse = lax.rsqrt(lax.optimization_barrier(jnp.mean(head_split * head_split, -1, keepdims=True)) + EPSILON)
    return (head_split * inverse, inverse)

def head_norm_back(grad_hat, normal, inverse):
    upstream = grad_hat.astype(jnp.float32)
    result = inverse * (upstream - normal * lax.optimization_barrier(jnp.mean(upstream * normal, -1, keepdims=True)))
    return result.reshape(result.shape[:-2] + (-1,))

def to_rows(array_in):
    leading, length, columns = array_in.shape
    return array_in.reshape(leading, length, columns // DH, DH).transpose(0, 2, 1, 3).reshape(-1, length, DH)

def from_rows(array_in, leading):
    stacked, length, depth = array_in.shape
    return array_in.reshape(leading, stacked // leading, length, depth).transpose(0, 2, 1, 3).reshape(leading, length, -1)

def reference(fine_input, conv_weight, conv_bias, norm_gain, query_weight, key_weight, value_weight, out_weight, cotangent):
    samples, fine_rows, channels = fine_input.shape
    tokens = fine_rows // 2
    features = conv_weight.shape[2]
    score_scale = SCORE_GAIN / math.sqrt(DH)
    paired = fine_input.reshape(samples, tokens, 2 * channels)
    zero_pair = jnp.zeros((samples, 1, 2 * channels), fine_input.dtype)
    padded = jnp.concatenate([zero_pair, paired, zero_pair], 1)
    low_taps = conv_weight[0:2].reshape(2 * channels, features)
    mid_taps = conv_weight[2:4].reshape(2 * channels, features)
    top_taps = conv_weight[4]
    preact = conv_bias + matmul(padded[:, :-2], low_taps) + matmul(padded[:, 1:-1], mid_taps) + matmul(padded[:, 2:, :channels], top_taps)
    active, gelu_slope = gelu_parts(preact)
    hidden = active.astype(jnp.bfloat16)
    hidden_f = hidden.astype(jnp.float32)
    row_inv = lax.rsqrt(lax.optimization_barrier(jnp.mean(hidden_f * hidden_f, -1, keepdims=True)) + EPSILON)
    normed = (hidden_f * row_inv * norm_gain).astype(jnp.bfloat16)
    query_n, query_inv = head_norm(matmul(normed, query_weight))
    key_n, key_inv = head_norm(matmul(normed, key_weight))
    values = matmul(normed, value_weight).astype(jnp.bfloat16)
    query_hat = query_n.astype(jnp.bfloat16).reshape(samples, tokens, -1)
    key_hat = key_n.astype(jnp.bfloat16).reshape(samples, tokens, -1)
    query_rows = to_rows(query_hat)
    key_rows = to_rows(key_hat)
    value_rows = to_rows(values)

    def forward_head(operands):
        query_head, key_head, value_head = operands
        scores = jnp.dot(query_head, key_head.T, preferred_element_type=jnp.float32) * score_scale
        exp_scores = jnp.exp(scores)
        totals = lax.optimization_barrier(jnp.sum(exp_scores, -1))
        numerator = jnp.dot(exp_scores.astype(jnp.bfloat16), value_head, preferred_element_type=jnp.float32)
        return ((numerator / totals[:, None]).astype(jnp.bfloat16), totals)
    attended_rows, total_rows = lax.map(forward_head, (query_rows, key_rows, value_rows))
    attended = from_rows(attended_rows, samples)
    section_out = (hidden_f + matmul(attended, out_weight)).astype(jnp.bfloat16)
    grad_scale = 1.0 / math.sqrt(samples * tokens)
    att_grad = matmul_t(cotangent, out_weight).astype(jnp.bfloat16)
    delta = lax.optimization_barrier(jnp.sum((att_grad.astype(jnp.float32) * attended.astype(jnp.float32)).reshape(samples, tokens, -1, DH), -1))
    grad_rows = to_rows(att_grad)
    delta_rows = delta.transpose(0, 2, 1).reshape(-1, tokens)

    def backward_head(operands):
        query_head, key_head, value_head, grad_head, total_head, delta_head = operands
        scores = jnp.dot(query_head, key_head.T, preferred_element_type=jnp.float32) * score_scale
        prob = jnp.exp(scores) / total_head[:, None]
        value_back = jnp.dot(prob.astype(jnp.bfloat16).T, grad_head, preferred_element_type=jnp.float32).astype(jnp.bfloat16)
        prob_grad = jnp.dot(grad_head, value_head.T, preferred_element_type=jnp.float32)
        score_back = (prob * (prob_grad - delta_head[:, None]) * score_scale).astype(jnp.bfloat16)
        query_up = jnp.dot(score_back, key_head, preferred_element_type=jnp.float32).astype(jnp.bfloat16)
        key_up = jnp.dot(score_back.T, query_head, preferred_element_type=jnp.float32).astype(jnp.bfloat16)
        return (query_up, key_up, value_back)
    query_up_rows, key_up_rows, value_back_rows = lax.map(backward_head, (query_rows, key_rows, value_rows, grad_rows, total_rows, delta_rows))
    value_back = from_rows(value_back_rows, samples)
    query_upstream = from_rows(query_up_rows, samples).reshape(samples, tokens, -1, DH)
    key_upstream = from_rows(key_up_rows, samples).reshape(samples, tokens, -1, DH)
    query_back = head_norm_back(query_upstream, query_n, query_inv).astype(jnp.bfloat16)
    key_back = head_norm_back(key_upstream, key_n, key_inv).astype(jnp.bfloat16)
    value_grad = jnp.dot(value_back.reshape(-1, value_back.shape[-1]).T, normed.reshape(-1, features), preferred_element_type=jnp.float32) * grad_scale
    norm_back = matmul_t(query_back, query_weight) + matmul_t(key_back, key_weight) + matmul_t(value_back, value_weight)
    gain_back = norm_back * norm_gain
    hidden_back = cotangent.astype(jnp.float32) + row_inv * (gain_back - hidden_f * row_inv * row_inv * lax.optimization_barrier(jnp.mean(gain_back * hidden_f, -1, keepdims=True)))
    pre_back = (hidden_back * gelu_slope).astype(jnp.bfloat16)
    zero_row = jnp.zeros((samples, 1, features), jnp.bfloat16)
    back_pad = jnp.concatenate([zero_row, pre_back, zero_row], 1)
    pair_grad = matmul_t(back_pad[:, 2:], low_taps) + matmul_t(back_pad[:, 1:-1], mid_taps)
    top_grad = matmul_t(back_pad[:, :-2], top_taps)
    pair_grad = pair_grad + jnp.concatenate([top_grad, jnp.zeros_like(top_grad)], -1)
    input_grad = pair_grad.astype(jnp.bfloat16).reshape(samples, fine_rows, channels)
    return (section_out, input_grad, value_grad)
```

```python
import functools
import math

import jax
import jax.numpy as jnp
from jax import lax
from jax.experimental import pallas as pl
from jax.experimental.pallas import tpu as pltpu
from jax.sharding import PartitionSpec as P

DH = 192
EPSILON = 1e-06
SCORE_GAIN = 3.0
GELU_ROOT = 0.7978845608028654
GELU_CUBIC = 0.044715
F32 = jnp.float32
BF16 = jnp.bfloat16
HALO_ROWS = 16
CHUNK = 16
VMEM_BYTES = 50 * 1024 * 1024


def spec(*_):
    return pl.BlockSpec(memory_space=pltpu.VMEM)


def anywhere():
    return pl.BlockSpec(memory_space=pl.ANY)


def params(limit=VMEM_BYTES):
    return pltpu.CompilerParams(vmem_limit_bytes=limit)


def cost(flops, nbytes):
    return pl.CostEstimate(flops=int(flops), bytes_accessed=int(nbytes), transcendentals=0)


def dot(left, right):
    return jnp.dot(left, right, preferred_element_type=F32)


def dot_rt(left, right):
    return lax.dot_general(left, right, (((1,), (1,)), ((), ())), preferred_element_type=F32)


def dot_lt(left, right):
    return lax.dot_general(left, right, (((0,), (0,)), ((), ())), preferred_element_type=F32)


def pick(shape, test):
    row = lax.broadcasted_iota(jnp.int32, shape, 0)
    col = lax.broadcasted_iota(jnp.int32, shape, 1)
    return jnp.where(test(row, col), 1.0, 0.0).astype(BF16)


def conv_kernel(pieces, tok, taps, *refs):
    fine_refs, side_refs = refs[:pieces], refs[pieces : 2 * pieces]
    weight_ref, out_ref, lhs = refs[2 * pieces :]
    channels = fine_refs[0].shape[1]
    fine_rows = 2 * tok

    @pl.when(pl.program_id(0) == 0)
    def _():
        for i in range(pieces):
            block = jnp.concatenate([fine_refs[i][...], side_refs[i][tok : tok + HALO_ROWS, :]], 0)
            for k in range(taps):

                def test(row, col, k=k):
                    want = 2 * row + k - 2
                    inside = (want >= 0) & (want < fine_rows)
                    spare = jnp.where(want < 0, fine_rows + 2 + want, want + 2)
                    return col == jnp.where(inside, want, spare)

                rows = dot(pick((tok, fine_rows + HALO_ROWS), test), block)
                lhs[i * tok : (i + 1) * tok, k * channels : (k + 1) * channels] = rows.astype(BF16)

    out_ref[...] = dot(lhs[...], weight_ref[...]).astype(BF16)


def conv_partial(fines, sides, weight, tok, taps):
    pieces = len(fines)
    depth, features = weight.shape
    tile = features // 3
    rows = pieces * tok
    whole = lambda a: pl.BlockSpec(a.shape, lambda i: (0, 0))
    return pl.pallas_call(
        functools.partial(conv_kernel, pieces, tok, taps),
        grid=(3,),
        out_shape=jax.ShapeDtypeStruct((rows, features), BF16),
        in_specs=[whole(a) for a in fines]
        + [whole(a) for a in sides]
        + [pl.BlockSpec((depth, tile), lambda i: (0, i))],
        out_specs=pl.BlockSpec((rows, tile), lambda i: (0, i)),
        scratch_shapes=[pltpu.VMEM((rows, depth), BF16)],
        compiler_params=params(),
        cost_estimate=cost(2 * rows * depth * features, 2 * depth * features),
        name="conv_partial",
    )(*fines, *sides, weight)


def gelu_value(preact):
    tangent = jnp.tanh(GELU_ROOT * (preact + GELU_CUBIC * preact * preact * preact))
    return 0.5 * preact * (1.0 + tangent), tangent


def head_scale(value):
    lane = lax.broadcasted_iota(jnp.int32, value.shape, 1)
    square = value * value
    parts = value.shape[1] // DH
    scale = jnp.zeros_like(value)
    for h in range(parts):
        here = (lane >= h * DH) & (lane < (h + 1) * DH)
        mean = jnp.sum(jnp.where(here, square, 0.0), -1, keepdims=True) * (1.0 / DH)
        scale = jnp.where(here, lax.rsqrt(mean + EPSILON), scale)
    return scale


def head_mean(value):
    lane = lax.broadcasted_iota(jnp.int32, value.shape, 1)
    parts = value.shape[1] // DH
    out = jnp.zeros_like(value)
    for h in range(parts):
        here = (lane >= h * DH) & (lane < (h + 1) * DH)
        mean = jnp.sum(jnp.where(here, value, 0.0), -1, keepdims=True) * (1.0 / DH)
        out = jnp.where(here, mean, out)
    return out


def post_kernel(own, place_ref, mine_ref, theirs_ref, bias_ref, gain_ref, wq_any, wk_any, wv_any, *refs):
    if own:
        qkv_ref, slice_ref, proj_ref, normed, wq, wk, wv, sems = refs
    else:
        qkv_ref, slice_ref, normed, wq, wk, wv, sems = refs
    copies = [
        pltpu.make_async_copy(a, b, sems.at[i])
        for i, (a, b) in enumerate(((wq_any, wq), (wk_any, wk), (wv_any, wv)))
    ]
    for c in copies:
        c.start()
    rows = mine_ref.shape[0]

    @pl.loop(0, rows // CHUNK)
    def _(i):
        at = pl.ds(pl.multiple_of(i * CHUNK, CHUNK), CHUNK)
        preact = mine_ref[at, :].astype(F32) + theirs_ref[at, :].astype(F32) + bias_ref[...]
        hidden = gelu_value(preact)[0].astype(BF16).astype(F32)
        inv = lax.rsqrt(jnp.mean(hidden * hidden, -1, keepdims=True) + EPSILON)
        normed[at, :] = (hidden * inv * gain_ref[...]).astype(BF16)

    features, width = wq.shape
    count = slice_ref.shape[1]
    start = place_ref[0] * count
    value = normed[...]
    slice_ref[...] = dot(value, pick((features, count), lambda r, c: r == c + start)).astype(BF16)
    for i, w in enumerate((wq, wk, wv)):
        copies[i].wait()
        proj = dot(value, w[...])
        if own and i < 2:
            proj_ref[:, i * width : (i + 1) * width] = proj
        if i < 2:
            proj = proj * head_scale(proj)
        qkv_ref[:, i * width : (i + 1) * width] = proj.astype(BF16)


def post(own, place, mine, theirs, bias, gain, wq, wk, wv, count):
    rows, features = mine.shape
    width = wq.shape[1]
    outs = [
        jax.ShapeDtypeStruct((rows, 3 * width), BF16),
        jax.ShapeDtypeStruct((rows, count), BF16),
    ]
    if own:
        outs.append(jax.ShapeDtypeStruct((rows, 2 * width), F32))
    return pl.pallas_call(
        functools.partial(post_kernel, own),
        out_shape=outs,
        in_specs=[pl.BlockSpec(memory_space=pltpu.SMEM)] + [spec()] * 4 + [anywhere()] * 3,
        out_specs=[spec()] * len(outs),
        scratch_shapes=[pltpu.VMEM((rows, features), BF16)]
        + [pltpu.VMEM((features, width), BF16)] * 3
        + [pltpu.SemaphoreType.DMA((3,))],
        compiler_params=params(),
        cost_estimate=cost(6 * rows * features * width, 6 * features * width),
        name="post",
    )(place, mine, theirs, bias, gain, wq, wk, wv)


def attention_kernel(tok, tile, heads, qkv_rows, grad_rows, *refs):
    groups, parts = len(qkv_rows), len(grad_rows)
    qkv_in, grad_in = refs[:groups], refs[groups : groups + parts]
    proj_ref, wq_any, wk_any, wv_any, wo_any, both_ref, dv_ref = refs[groups + parts : groups + parts + 7]
    qkv, grad, dv_acc, dk_acc, dq_acc, att, wq, wk, wv, wo, sems = refs[groups + parts + 7 :]
    width = heads * DH
    total = qkv.shape[0]
    step, steps = pl.program_id(0), pl.num_programs(0)
    loads, weights = [], []
    at = 0
    for i, rows in enumerate(qkv_rows):
        loads.append(pltpu.make_async_copy(qkv_in[i], qkv.at[pl.ds(at, rows)], sems.at[len(loads)]))
        at += rows
    at = 0
    for i, rows in enumerate(grad_rows):
        source = grad_in[i].at[pl.ds(0, rows)]
        loads.append(pltpu.make_async_copy(source, grad.at[pl.ds(at, rows)], sems.at[len(loads)]))
        at += rows
    for a, b in ((wo_any, wo), (wq_any, wq), (wk_any, wk), (wv_any, wv)):
        weights.append(pltpu.make_async_copy(a, b, sems.at[len(loads) + len(weights)]))

    @pl.when(step == 0)
    def _():
        for c in loads:
            c.start()
        for c in weights:
            c.start()
        for c in loads:
            c.wait()
        dv_acc[...] = jnp.zeros_like(dv_acc)
        dk_acc[...] = jnp.zeros_like(dk_acc)

    scale = SCORE_GAIN / math.sqrt(DH)
    here = pl.ds(pl.multiple_of(step * tile, tile), tile)
    lanes = min(128, tile)
    for h in range(heads):
        cols = slice(h * DH, (h + 1) * DH)
        key = qkv[:, width + h * DH : width + (h + 1) * DH]
        val = qkv[:, 2 * width + h * DH : 2 * width + (h + 1) * DH]
        query = qkv[here, :][:, cols]
        up = grad[here, :][:, cols]
        expo = jnp.exp(dot_rt(key, query) * scale)
        back = dot_rt(val, up)
        inv = 1.0 / jnp.sum(expo, 0, keepdims=True)
        delta = jnp.sum(expo * back, 0, keepdims=True) * inv
        prob = expo * inv
        prob_b = prob.astype(BF16)
        dv_acc[:, cols] += dot(prob_b, up)
        score_own = (prob[:tok] * (back[:tok] - delta) * scale).astype(BF16)
        dk_acc[:, cols] += dot(score_own, query)

        @pl.when(step == 0)
        def _():
            att[:, cols] = dot_lt(prob_b[:, :lanes], val)[:tok].astype(BF16)
            score = (prob[:, :lanes] * (back[:, :lanes] - delta[:, :lanes]) * scale).astype(BF16)
            dq_acc[:, cols] = dot_lt(score, key)[:tok]

    @pl.when(step == steps - 1)
    def _():
        dv = dv_acc[...].astype(BF16)
        dv_ref[...] = dv
        for c in weights:
            c.wait()
        both_ref[:tok, :] = dot(att[...], wo[...]).astype(BF16)
        backs = []
        for acc, lo in ((dq_acc, 0), (dk_acc, width)):
            proj = proj_ref[:, lo : lo + width]
            inv = head_scale(proj)
            normal = proj * inv
            up = acc[...].astype(BF16).astype(F32)
            backs.append((inv * (up - normal * head_mean(up * normal))).astype(BF16))
        norm_back = dot_rt(backs[0], wq[...]) + dot_rt(backs[1], wk[...]) + dot_rt(dv[:tok], wv[...])
        both_ref[tok:, :] = norm_back.astype(BF16)


def attention(qkvs, grads, grad_rows, proj, wq, wk, wv, wo, tok):
    qkv_rows = tuple(a.shape[0] for a in qkvs)
    total = sum(qkv_rows)
    features, width = wq.shape
    heads = width // DH
    tile = 256 if total <= 2048 else 128
    copies = len(qkvs) + len(grads) + 4
    return pl.pallas_call(
        functools.partial(attention_kernel, tok, tile, heads, qkv_rows, tuple(grad_rows)),
        grid=(total // tile,),
        out_shape=[
            jax.ShapeDtypeStruct((2 * tok, features), BF16),
            jax.ShapeDtypeStruct((total, width), BF16),
        ],
        in_specs=[anywhere()] * (len(qkvs) + len(grads))
        + [pl.BlockSpec(proj.shape, lambda i: (0, 0))]
        + [anywhere()] * 4,
        out_specs=[
            pl.BlockSpec((2 * tok, features), lambda i: (0, 0)),
            pl.BlockSpec((total, width), lambda i: (0, 0)),
        ],
        scratch_shapes=[
            pltpu.VMEM((total, 3 * width), BF16),
            pltpu.VMEM((total, width), BF16),
            pltpu.VMEM((total, width), F32),
            pltpu.VMEM((tok, width), F32),
            pltpu.VMEM((tok, width), F32),
            pltpu.VMEM((tok, width), BF16),
            pltpu.VMEM((features, width), BF16),
            pltpu.VMEM((features, width), BF16),
            pltpu.VMEM((features, width), BF16),
            pltpu.VMEM((width, features), BF16),
            pltpu.SemaphoreType.DMA((copies,)),
        ],
        compiler_params=params(VMEM_BYTES if total <= 2048 else VMEM_BYTES + VMEM_BYTES // 5),
        cost_estimate=cost(6 * total * total * width, 8 * total * width),
        name="attention",
    )(*qkvs, *grads, proj, wq, wk, wv, wo)


def finish_kernel(mine_ref, theirs_ref, bias_ref, gain_ref, cot_ref, here_ref, there_ref, out_ref, pre_ref, head_ref, tail_ref):
    tok = out_ref.shape[0]

    @pl.loop(0, tok // CHUNK)
    def _(i):
        at = pl.ds(pl.multiple_of(i * CHUNK, CHUNK), CHUNK)
        low = pl.ds(pl.multiple_of(tok + i * CHUNK, CHUNK), CHUNK)
        preact = mine_ref[at, :].astype(F32) + theirs_ref[at, :].astype(F32) + bias_ref[...]
        active, tangent = gelu_value(preact)
        slope = 0.5 * (1.0 + tangent) + 0.5 * preact * (1.0 - tangent * tangent) * GELU_ROOT * (
            1.0 + 3.0 * GELU_CUBIC * preact * preact
        )
        hidden = active.astype(BF16).astype(F32)
        inv = lax.rsqrt(jnp.mean(hidden * hidden, -1, keepdims=True) + EPSILON)
        attended = here_ref[at, :].astype(F32) + there_ref[at, :].astype(F32)
        out_ref[at, :] = (hidden + attended).astype(BF16)
        gain_back = (here_ref[low, :].astype(F32) + there_ref[low, :].astype(F32)) * gain_ref[...]
        mean = jnp.mean(gain_back * hidden, -1, keepdims=True)
        back = cot_ref[at, :].astype(F32) + inv * (gain_back - hidden * (inv * inv * mean))
        pre_ref[at, :] = (back * slope).astype(BF16)

    head_ref[...] = pre_ref[0:1, :]
    tail_ref[...] = pre_ref[tok - 1 : tok, :]


def finish(mine, theirs, bias, gain, cot, here, there):
    tok, features = cot.shape
    row = jax.ShapeDtypeStruct((1, features), BF16)
    full = jax.ShapeDtypeStruct((tok, features), BF16)
    return pl.pallas_call(
        finish_kernel,
        out_shape=[full, full, row, row],
        in_specs=[spec()] * 7,
        out_specs=[spec()] * 4,
        compiler_params=params(),
        cost_estimate=cost(40 * tok * features, 12 * tok * features),
        name="finish",
    )(mine, theirs, bias, gain, cot, here, there)


def conv_back_kernel(order, pre_ref, before_ref, after_ref, weight_ref, out_ref, acc):
    step = pl.program_id(0)
    tok = pre_ref.shape[0]
    channels = weight_ref.shape[1]
    pre = pre_ref[...]
    for i, k in enumerate(order):

        @pl.when(step == i)
        def _(k=k):
            if k < 2:
                left = jnp.concatenate([pre[1:], after_ref[...]], 0)
            elif k < 4:
                left = pre
            else:
                left = jnp.concatenate([before_ref[...], pre[:-1]], 0)
            value = dot_rt(left, weight_ref[0])
            cols = slice((k % 2) * channels, (k % 2 + 1) * channels)
            if k in (2, 3):
                acc[:, cols] = value
            else:
                acc[:, cols] += value

    @pl.when(step == len(order) - 1)
    def _():
        even = pick((2 * tok, tok), lambda r, c: r == 2 * c)
        odd = pick((2 * tok, tok), lambda r, c: r == 2 * c + 1)
        rows = dot(even, acc[:, :channels].astype(BF16)) + dot(odd, acc[:, channels:].astype(BF16))
        out_ref[...] = rows.astype(BF16)


def conv_back(pre, before, after, weight):
    tok, features = pre.shape
    taps, channels = weight.shape[:2]
    order = (2, 3, 0, 1, 4)
    whole = lambda a: pl.BlockSpec(a.shape, lambda i: (0, 0))
    return pl.pallas_call(
        functools.partial(conv_back_kernel, order),
        grid=(taps,),
        out_shape=jax.ShapeDtypeStruct((2 * tok, channels), BF16),
        in_specs=[whole(pre), whole(before), whole(after)]
        + [
            pl.BlockSpec(
                (1, channels, features),
                lambda i: (jnp.where(i < 2, i + 2, jnp.where(i < 4, i - 2, 4)), 0, 0),
            )
        ],
        out_specs=pl.BlockSpec((2 * tok, channels), lambda i: (0, 0)),
        scratch_shapes=[pltpu.VMEM((tok, 2 * channels), F32)],
        compiler_params=params(),
        cost_estimate=cost(2 * tok * taps * channels * features, 2 * taps * channels * features),
        name="conv_back",
    )(pre, before, after, weight)


def value_kernel(rows_of, scale, dv_ref, *refs):
    slices, out_ref = refs[:-1], refs[-1]
    total, at = None, 0
    for ref, rows in zip(slices, rows_of):
        term = dot_lt(dv_ref[at : at + rows, :], ref[...])
        total = term if total is None else total + term
        at += rows
    out_ref[...] = total * scale


def value_gradient(dv, slices, scale):
    rows_of = tuple(a.shape[0] for a in slices)
    return pl.pallas_call(
        functools.partial(value_kernel, rows_of, scale),
        out_shape=jax.ShapeDtypeStruct((dv.shape[1], slices[0].shape[1]), F32),
        in_specs=[spec()] * (1 + len(slices)),
        out_specs=spec(),
        compiler_params=params(),
        cost_estimate=cost(2 * dv.shape[0] * dv.shape[1] * 192, 2 * dv.size),
        name="value_gradient",
    )(dv, *slices)


def on_device(
    fine_input,
    conv_weight,
    conv_bias,
    norm_gain,
    query_weight,
    key_weight,
    value_weight,
    out_weight,
    cotangent,
):
    samples, fine_rows, channels = fine_input.shape
    tok = fine_rows // 2
    taps, _, features = conv_weight.shape
    n = lax.axis_size("seq")
    grad_scale = 1.0 / math.sqrt(samples * tok * n)
    up = [(i, i + 1) for i in range(n - 1)]
    down = [(j, i) for i, j in up]
    cycle = list(range(0, n, 2)) + list(range(n - 1, 0, -2))
    ahead = [(cycle[i], cycle[(i + 1) % n]) for i in range(n)]
    behind = [(j, i) for i, j in ahead]
    swap = [(0, 1), (1, 0)]
    place = lax.axis_index("seq").astype(jnp.int32).reshape(1)
    bias, gain = conv_bias.reshape(1, features), norm_gain.reshape(1, features)
    flat_weight = conv_weight.reshape(taps * channels, features)
    fine, cot = fine_input[0], cotangent[0]

    before = lax.ppermute(fine[-2:], "seq", up)
    after = lax.ppermute(fine[:1], "seq", down)
    att_grad = dot_rt(cot, out_weight).astype(BF16)
    pad = jnp.zeros((HALO_ROWS - 3, channels), BF16)
    side = jnp.concatenate([att_grad, before, after, pad], 0)

    fine_groups, side_groups = [[fine]], [[side]]
    f_cw = f_ccw = fine
    s_cw = s_ccw = side
    half = n // 2
    side_cut = (side.shape[0] // 2 + 15) // 16 * 16
    for k in range(1, half + 1):
        if k < half:
            f_cw, f_ccw = lax.ppermute(f_cw, "seq", ahead), lax.ppermute(f_ccw, "seq", behind)
            s_cw, s_ccw = lax.ppermute(s_cw, "seq", ahead), lax.ppermute(s_ccw, "seq", behind)
            fine_groups.append([f_cw, f_ccw])
            side_groups.append([s_cw, s_ccw])
        else:
            f_a, f_b = lax.ppermute(f_cw[:tok], "seq", ahead), lax.ppermute(f_ccw[tok:], "seq", behind)
            s_a = lax.ppermute(s_cw[:side_cut], "seq", ahead)
            s_b = lax.ppermute(s_ccw[side_cut:], "seq", behind)
            fine_groups.append([jnp.concatenate([f_a, f_b], 0)])
            side_groups.append([jnp.concatenate([s_a, s_b], 0)])

    qkvs, slices = [], []
    for g, (fines, sides) in enumerate(zip(fine_groups, side_groups)):
        mine = conv_partial(fines, sides, flat_weight, tok, taps)
        theirs = lax.ppermute(mine, "wide", swap)
        outs = post(g == 0, place, mine, theirs, bias, gain, query_weight, key_weight, value_weight, features // n)
        qkvs.append(outs[0])
        slices.append(outs[1])
        if g == 0:
            proj, own_mine, own_theirs = outs[2], mine, theirs

    grads = [a for sides in side_groups for a in sides]
    both, dv = attention(
        qkvs, grads, [tok] * len(grads), proj, query_weight, key_weight, value_weight, out_weight, tok
    )
    there = lax.ppermute(both, "wide", swap)
    value_grad = value_gradient(dv, slices, grad_scale)
    section_out, pre_back, head, tail = finish(own_mine, own_theirs, bias, gain, cot, both, there)
    pre_before = lax.ppermute(tail, "seq", up)
    pre_after = lax.ppermute(head, "seq", down)
    input_grad = conv_back(pre_back, pre_before, pre_after, conv_weight)
    return (section_out[None], input_grad[None], value_grad)


def solution(mesh):
    in_specs = (
        P("groups", "seq", "wide"),
        P(None, "wide", None),
        P(),
        P(),
        P(None, "wide"),
        P(None, "wide"),
        P(None, "wide"),
        P("wide", None),
        P("groups", "seq", None),
    )
    out_specs = (P("groups", "seq", None), P("groups", "seq", "wide"), P(("groups", "wide"), "seq"))
    return jax.shard_map(
        on_device, mesh=mesh, in_specs=in_specs, out_specs=out_specs, check_vma=False
    )
```

```python
import functools
import math

import jax
import jax.numpy as jnp
from jax import lax
from jax.experimental import pallas as pl
from jax.experimental.pallas import tpu as pltpu
from jax.sharding import PartitionSpec as P

DH = 192
EPSILON = 1e-06
SCORE_GAIN = 3.0
GELU_ROOT = 0.7978845608028654
GELU_CUBIC = 0.044715
F32 = jnp.float32
BF16 = jnp.bfloat16
HALO_ROWS = 16
CHUNK = 16
SMEM = pl.BlockSpec(memory_space=pltpu.SMEM)
MIB = 1024 * 1024


def spec():
    return pl.BlockSpec(memory_space=pltpu.VMEM)


def in_hbm():
    return pl.BlockSpec(memory_space=pltpu.HBM)


def anywhere():
    return pl.BlockSpec(memory_space=pl.ANY)


def far(value):
    return pltpu.with_memory_space_constraint(value, pltpu.HBM)


def near_core(value):
    return pltpu.with_memory_space_constraint(value, pltpu.VMEM)


def params(limit=8):
    return pltpu.CompilerParams(vmem_limit_bytes=limit * MIB)


def cost(flops, nbytes):
    return pl.CostEstimate(flops=int(flops), bytes_accessed=int(nbytes), transcendentals=0)


def dot(left, right):
    return jnp.dot(left, right, preferred_element_type=F32)


def dot_rt(left, right):
    return lax.dot_general(left, right, (((1,), (1,)), ((), ())), preferred_element_type=F32)


def dot_lt(left, right):
    return lax.dot_general(left, right, (((0,), (0,)), ((), ())), preferred_element_type=F32)


def pick(shape, test):
    row = lax.broadcasted_iota(jnp.int32, shape, 0)
    col = lax.broadcasted_iota(jnp.int32, shape, 1)
    return jnp.where(test(row, col), 1.0, 0.0).astype(BF16)


def edges_kernel(fine_any, fine_ref, edge_ref, sem):
    copy = pltpu.make_async_copy(fine_any, fine_ref, sem)
    copy.start()
    copy.wait()
    rows = fine_ref.shape[0]
    edge_ref[0:2, :] = fine_ref[rows - 2 :, :]
    edge_ref[2:3, :] = fine_ref[0:1, :]


def edges(fine):
    return pl.pallas_call(
        edges_kernel,
        out_shape=[
            jax.ShapeDtypeStruct(fine.shape, BF16),
            jax.ShapeDtypeStruct((3, fine.shape[1]), BF16),
        ],
        in_specs=[in_hbm()],
        out_specs=[spec()] * 2,
        scratch_shapes=[pltpu.SemaphoreType.DMA],
        compiler_params=params(),
        cost_estimate=cost(fine.size, 2 * fine.size),
        name="edges",
    )(far(fine))


def sided(place_ref, first_ref, second_ref, before_rows):
    even = place_ref[0] % 2 == 0
    first, second = first_ref[...].astype(F32), second_ref[...].astype(F32)
    low = lax.broadcasted_iota(jnp.int32, first.shape, 0) < before_rows
    return jnp.where(low == even, second, first).astype(BF16)


def early_kernel(cot_any, wo_any, grad_ref, cot, wo, sems):
    copies = [
        pltpu.make_async_copy(cot_any, cot, sems.at[0]),
        pltpu.make_async_copy(wo_any, wo, sems.at[1]),
    ]
    for c in copies:
        c.start()
    for c in copies:
        c.wait()
    grad_ref[...] = dot_rt(cot[...], wo[...]).astype(BF16)


def early(cot, wo):
    tok, features = cot.shape
    width = wo.shape[0]
    return pl.pallas_call(
        early_kernel,
        out_shape=jax.ShapeDtypeStruct((tok, width), BF16),
        in_specs=[in_hbm()] * 2,
        out_specs=spec(),
        scratch_shapes=[
            pltpu.VMEM((tok, features), BF16),
            pltpu.VMEM(wo.shape, BF16),
            pltpu.SemaphoreType.DMA((2,)),
        ],
        compiler_params=params(),
        cost_estimate=cost(2 * tok * features * width, 2 * wo.size),
        name="early",
    )(far(cot), far(wo))


def conv_kernel(order, place_ref, fine_ref, first_ref, second_ref, taps_any, out_ref, taps, sems):
    fine_rows, channels = fine_ref.shape
    tok = fine_rows // 2
    copies = {k: pltpu.make_async_copy(taps_any.at[k], taps.at[k], sems.at[k]) for k in order}
    for k in order:
        copies[k].start()
    side = sided(place_ref, first_ref, second_ref, 2)
    spare_rows = jnp.zeros((HALO_ROWS - side.shape[0], channels), BF16)
    block = jnp.concatenate([fine_ref[...], side, spare_rows], 0)
    total = None
    for k in order:

        def test(row, col, k=k):
            want = 2 * row + k - 2
            inside = (want >= 0) & (want < fine_rows)
            spare = jnp.where(want < 0, fine_rows + 2 + want, want + 2)
            return col == jnp.where(inside, want, spare)

        rows = dot(pick((tok, fine_rows + HALO_ROWS), test), block).astype(BF16)
        copies[k].wait()
        term = dot(rows, taps[k])
        total = term if total is None else total + term
    out_ref[...] = total.astype(BF16)


def conv_partial(place, fine, first, second, weight):
    taps, channels, features = weight.shape
    tok = fine.shape[0] // 2
    return pl.pallas_call(
        functools.partial(conv_kernel, tuple(range(taps))),
        out_shape=jax.ShapeDtypeStruct((tok, features), BF16),
        in_specs=[SMEM] + [spec()] * 3 + [in_hbm()],
        out_specs=spec(),
        scratch_shapes=[pltpu.VMEM(weight.shape, BF16), pltpu.SemaphoreType.DMA((taps,))],
        compiler_params=params(12),
        cost_estimate=cost(2 * tok * weight.size, 2 * weight.size),
        name="conv_partial",
    )(place, fine, first, second, far(weight))


def gelu_value(preact):
    tangent = jnp.tanh(GELU_ROOT * (preact + GELU_CUBIC * preact * preact * preact))
    return 0.5 * preact * (1.0 + tangent), tangent


def head_scale(value):
    lane = lax.broadcasted_iota(jnp.int32, value.shape, 1)
    square = value * value
    parts = value.shape[1] // DH
    scale = jnp.zeros_like(value)
    for h in range(parts):
        here = (lane >= h * DH) & (lane < (h + 1) * DH)
        mean = jnp.sum(jnp.where(here, square, 0.0), -1, keepdims=True) * (1.0 / DH)
        scale = jnp.where(here, lax.rsqrt(mean + EPSILON), scale)
    return scale


def head_mean(value):
    lane = lax.broadcasted_iota(jnp.int32, value.shape, 1)
    parts = value.shape[1] // DH
    out = jnp.zeros_like(value)
    for h in range(parts):
        here = (lane >= h * DH) & (lane < (h + 1) * DH)
        mean = jnp.sum(jnp.where(here, value, 0.0), -1, keepdims=True) * (1.0 / DH)
        out = jnp.where(here, mean, out)
    return out


def norm_kernel(wide_ref, mine_ref, theirs_ref, bias_ref, gain_ref, *refs):
    weights_any, (grad_ref, normed_ref, message_ref), weights, sems = refs[:3], refs[3:6], refs[6:9], refs[9]
    tok, features = mine_ref.shape
    width = message_ref.shape[1]
    half = tok // 2
    copies = [pltpu.make_async_copy(weights_any[i], weights[i], sems.at[i]) for i in range(3)]
    for c in copies:
        c.start()

    @pl.loop(0, tok // CHUNK)
    def _(i):
        at = pl.ds(pl.multiple_of(i * CHUNK, CHUNK), CHUNK)
        preact = mine_ref[at, :].astype(F32) + theirs_ref[at, :].astype(F32) + bias_ref[...]
        hidden = gelu_value(preact)[0].astype(BF16).astype(F32)
        inv = lax.rsqrt(jnp.mean(hidden * hidden, -1, keepdims=True) + EPSILON)
        normed_ref[at, :] = (hidden * inv * gain_ref[...]).astype(BF16)

    own = normed_ref[pl.ds(pl.multiple_of(wide_ref[0] * half, CHUNK), half), :]
    for j in range(features // width):
        message_ref[j * half : (j + 1) * half, :] = own[:, j * width : (j + 1) * width]
    message_ref[features // width * half :, :] = grad_ref[...]
    for c in copies:
        c.wait()


def norm(wide, mine, theirs, bias, gain, weights, grad):
    tok, features = mine.shape
    width = weights[0].shape[1]
    rows = features // width * (tok // 2) + tok
    return pl.pallas_call(
        norm_kernel,
        out_shape=[
            jax.ShapeDtypeStruct((tok, features), BF16),
            jax.ShapeDtypeStruct((rows, width), BF16),
        ]
        + [pltpu.VMEM(w.shape, BF16) for w in weights],
        in_specs=[SMEM] + [spec()] * 4 + [in_hbm()] * 3 + [spec()],
        out_specs=[spec()] * 5,
        scratch_shapes=[pltpu.SemaphoreType.DMA((3,))],
        compiler_params=params(),
        cost_estimate=cost(30 * tok * features, 6 * tok * features),
        name="norm",
    )(wide, mine, theirs, bias, gain, *[far(w) for w in weights], grad)


def project(value, place_ref, weights, qkv_ref, slice_ref, proj_ref=None):
    features, width = weights[0].shape
    count = slice_ref.shape[1]
    start = place_ref[0] * count
    slice_ref[...] = dot(value, pick((features, count), lambda r, c: r == c + start)).astype(BF16)
    for i, w in enumerate(weights):
        proj = dot(value, w[...])
        if proj_ref is not None and i < 2:
            proj_ref[:, i * width : (i + 1) * width] = proj
        if i < 2:
            proj = proj * head_scale(proj)
        qkv_ref[:, i * width : (i + 1) * width] = proj.astype(BF16)


def own_kernel(place_ref, normed_ref, grad_ref, wq_ref, wk_ref, wv_ref, qkv_ref, slice_ref, proj_ref):
    qkv_ref[:, 3 * wq_ref.shape[1] :] = grad_ref[...]
    project(normed_ref[...], place_ref, (wq_ref, wk_ref, wv_ref), qkv_ref, slice_ref, proj_ref)


def own_project(place, normed, grad, wq, wk, wv, count):
    rows, features = normed.shape
    width = wq.shape[1]
    return pl.pallas_call(
        own_kernel,
        out_shape=[
            jax.ShapeDtypeStruct((rows, 4 * width), BF16),
            jax.ShapeDtypeStruct((rows, count), BF16),
            jax.ShapeDtypeStruct((rows, 2 * width), F32),
        ],
        in_specs=[SMEM] + [spec()] * 5,
        out_specs=[spec()] * 3,
        compiler_params=params(),
        cost_estimate=cost(6 * rows * features * width, 6 * features * width),
        name="own_project",
    )(place, normed, grad, wq, wk, wv)


def others_kernel(count, half, place_ref, wide_ref, *refs):
    mine, theirs = refs[:count], refs[count : 2 * count]
    wq_ref, wk_ref, wv_ref, qkv_ref, slice_ref, lhs = refs[2 * count :]
    width = wq_ref.shape[1]
    for b in range(count):
        for ref, core in ((mine[b], wide_ref[0]), (theirs[b], 1 - wide_ref[0])):
            row = pl.ds(pl.multiple_of(b * 2 * half + core * half, CHUNK), half)
            for j in range(wq_ref.shape[0] // width):
                lhs[row, j * width : (j + 1) * width] = ref[j * half : (j + 1) * half, :]
        base = b * 2 * half
        qkv_ref[base : base + 2 * half, 3 * width :] = mine[b][mine[b].shape[0] - 2 * half :, :]
    project(lhs[...], place_ref, (wq_ref, wk_ref, wv_ref), qkv_ref, slice_ref)


def others_project(place, wide, mine, theirs, wq, wk, wv, count, half):
    features, width = wq.shape
    rows = len(mine) * 2 * half
    return pl.pallas_call(
        functools.partial(others_kernel, len(mine), half),
        out_shape=[
            jax.ShapeDtypeStruct((rows, 4 * width), BF16),
            jax.ShapeDtypeStruct((rows, count), BF16),
        ],
        in_specs=[SMEM] * 2 + [spec()] * (2 * len(mine) + 3),
        out_specs=[spec()] * 2,
        scratch_shapes=[pltpu.VMEM((rows, features), BF16)],
        compiler_params=params(),
        cost_estimate=cost(6 * rows * features * width, 6 * features * width),
        name="others_project",
    )(place, wide, *mine, *theirs, wq, wk, wv)


def attention_kernel(tok, tile, heads, qkv_rows, *refs):
    groups = len(qkv_rows)
    width = heads * DH
    total = sum(qkv_rows)
    qkv_in = refs[:groups]
    proj_ref, wq, wk, wv, wo, both_ref, dv_ref = refs[groups : groups + 7]
    qkv, dv_acc, dk_acc, dq_acc, att, sems = refs[groups + 7 :]
    loads = []
    at = 0
    for i, rows in enumerate(qkv_rows):
        loads.append(pltpu.make_async_copy(qkv_in[i], qkv.at[pl.ds(at, rows)], sems.at[len(loads)]))
        at += rows
    for c in loads:
        c.start()
    for c in loads:
        c.wait()

    scale = SCORE_GAIN / math.sqrt(DH)
    lanes = min(128, tile)

    def block(start, first, h):
        here = pl.ds(start, tile)
        cols = slice(h * DH, (h + 1) * DH)
        key = qkv[:, width + h * DH : width + (h + 1) * DH]
        val = qkv[:, 2 * width + h * DH : 2 * width + (h + 1) * DH]
        query = qkv[here, cols]
        up = qkv[here, 3 * width + h * DH : 3 * width + (h + 1) * DH]
        expo = jnp.exp(dot_rt(key, query) * scale)
        back = dot_rt(val, up)
        inv = 1.0 / jnp.sum(expo, 0, keepdims=True)
        delta = jnp.sum(expo * back, 0, keepdims=True) * inv
        prob_b = (expo * inv).astype(BF16)
        score_own = (expo[:tok] * inv * (back[:tok] - delta) * scale).astype(BF16)
        if first:
            dv_acc[:, cols] = dot(prob_b, up)
            dk_acc[:, cols] = dot(score_own, query)
        else:
            dv_acc[:, cols] += dot(prob_b, up)
            dk_acc[:, cols] += dot(score_own, query)

        def own():
            att[:, cols] = dot_lt(prob_b[:, :lanes], val)[:tok].astype(BF16)
            score = expo[:, :lanes] * inv[:, :lanes] * (back[:, :lanes] - delta[:, :lanes]) * scale
            dq_acc[:, cols] = dot_lt(score.astype(BF16), key)[:tok]

        if first:
            own()
        elif first is None:
            pl.when(start == 0)(own)

    if total <= 2048:
        for step in range(total // tile):
            for h in range(heads):
                block(step * tile, step == 0, h)
    else:
        dv_acc[...] = jnp.zeros_like(dv_acc)
        dk_acc[...] = jnp.zeros_like(dk_acc)
        for h in range(heads):

            @pl.loop(0, total // tile)
            def _(step):
                block(pl.multiple_of(step * tile, tile), None, h)

    dv_ref[...] = dv_acc[...].astype(BF16)
    both_ref[:tok, :] = dot(att[...], wo[...]).astype(BF16)
    backs = []
    for acc, lo in ((dq_acc, 0), (dk_acc, width)):
        proj = proj_ref[:, lo : lo + width]
        inv = head_scale(proj)
        normal = proj * inv
        up = acc[...].astype(BF16).astype(F32)
        backs.append((inv * (up - normal * head_mean(up * normal))).astype(BF16))
    norm_back = dot_rt(backs[0], wq[...]) + dot_rt(backs[1], wk[...]) + dot_rt(dv_ref[:tok, :], wv[...])
    both_ref[tok:, :] = norm_back.astype(BF16)


def attention(qkvs, proj, wq, wk, wv, wo, tok):
    qkv_rows = tuple(a.shape[0] for a in qkvs)
    total = sum(qkv_rows)
    features, width = wq.shape
    heads = width // DH
    tile = 256 if total <= 2048 else 128
    return pl.pallas_call(
        functools.partial(attention_kernel, tok, tile, heads, qkv_rows),
        out_shape=[
            jax.ShapeDtypeStruct((2 * tok, features), BF16),
            jax.ShapeDtypeStruct((total, width), BF16),
        ],
        in_specs=[anywhere()] * len(qkvs) + [spec()] * 5,
        out_specs=[spec()] * 2,
        scratch_shapes=[
            pltpu.VMEM((total, 4 * width), BF16),
            pltpu.VMEM((total, width), F32),
            pltpu.VMEM((tok, width), F32),
            pltpu.VMEM((tok, width), F32),
            pltpu.VMEM((tok, width), BF16),
            pltpu.SemaphoreType.DMA((len(qkvs),)),
        ],
        compiler_params=params(24 if total <= 2048 else 56),
        cost_estimate=cost(6 * total * total * width, 8 * total * width),
        name="attention",
    )(*qkvs, proj, wq, wk, wv, wo)


def finish_kernel(mine_ref, theirs_ref, bias_ref, gain_ref, cot_ref, here_ref, there_ref, *refs):
    taps_any, out_ref, pre_ref, edge_ref, taps_ref, sem = refs
    tok = out_ref.shape[0]
    copy = pltpu.make_async_copy(taps_any, taps_ref, sem)
    copy.start()

    @pl.loop(0, tok // CHUNK)
    def _(i):
        at = pl.ds(pl.multiple_of(i * CHUNK, CHUNK), CHUNK)
        low = pl.ds(pl.multiple_of(tok + i * CHUNK, CHUNK), CHUNK)
        preact = mine_ref[at, :].astype(F32) + theirs_ref[at, :].astype(F32) + bias_ref[...]
        active, tangent = gelu_value(preact)
        slope = 0.5 * (1.0 + tangent) + 0.5 * preact * (1.0 - tangent * tangent) * GELU_ROOT * (
            1.0 + 3.0 * GELU_CUBIC * preact * preact
        )
        hidden = active.astype(BF16).astype(F32)
        inv = lax.rsqrt(jnp.mean(hidden * hidden, -1, keepdims=True) + EPSILON)
        attended = here_ref[at, :].astype(F32) + there_ref[at, :].astype(F32)
        out_ref[at, :] = (hidden + attended).astype(BF16)
        gain_back = (here_ref[low, :].astype(F32) + there_ref[low, :].astype(F32)) * gain_ref[...]
        mean = jnp.mean(gain_back * hidden, -1, keepdims=True)
        back = cot_ref[at, :].astype(F32) + inv * (gain_back - hidden * (inv * inv * mean))
        pre_ref[at, :] = (back * slope).astype(BF16)

    edge_ref[0:1, :] = pre_ref[tok - 1 : tok, :]
    edge_ref[1:2, :] = pre_ref[0:1, :]
    copy.wait()


def finish(mine, theirs, bias, gain, cot, here, there, taps):
    tok, features = cot.shape
    row = jax.ShapeDtypeStruct((2, features), BF16)
    full = jax.ShapeDtypeStruct((tok, features), BF16)
    return pl.pallas_call(
        finish_kernel,
        out_shape=[full, full, row, pltpu.VMEM(taps.shape, BF16)],
        in_specs=[spec()] * 7 + [in_hbm()],
        out_specs=[spec()] * 4,
        scratch_shapes=[pltpu.SemaphoreType.DMA],
        compiler_params=params(16),
        cost_estimate=cost(40 * tok * features, 12 * tok * features),
        name="finish",
    )(mine, theirs, bias, gain, cot, here, there, far(taps))


def back_mid_kernel(pre_ref, weight_ref, out_ref):
    channels = weight_ref.shape[1]
    pre = pre_ref[...]
    out_ref[:, :channels] = dot_rt(pre, weight_ref[2])
    out_ref[:, channels:] = dot_rt(pre, weight_ref[3])


def back_mid(pre, weight):
    tok, features = pre.shape
    channels = weight.shape[1]
    return pl.pallas_call(
        back_mid_kernel,
        out_shape=jax.ShapeDtypeStruct((tok, 2 * channels), F32),
        in_specs=[spec()] * 2,
        out_specs=spec(),
        compiler_params=params(),
        cost_estimate=cost(4 * tok * channels * features, 4 * channels * features),
        name="back_mid",
    )(pre, weight)


def back_rest_kernel(place_ref, pre_ref, mid_ref, first_ref, second_ref, weight_ref, out_ref):
    tok, channels = pre_ref.shape[0], weight_ref.shape[1]
    pre = pre_ref[...]
    side = sided(place_ref, first_ref, second_ref, 1)
    after = jnp.concatenate([pre[1:], side[1:2]], 0)
    before = jnp.concatenate([side[0:1], pre[:-1]], 0)
    first = mid_ref[:, :channels] + dot_rt(after, weight_ref[0]) + dot_rt(before, weight_ref[4])
    second = mid_ref[:, channels:] + dot_rt(after, weight_ref[1])
    even = pick((2 * tok, tok), lambda r, c: r == 2 * c)
    odd = pick((2 * tok, tok), lambda r, c: r == 2 * c + 1)
    out_ref[...] = (dot(even, first.astype(BF16)) + dot(odd, second.astype(BF16))).astype(BF16)


def back_rest(place, pre, mid, first, second, weight):
    tok, features = pre.shape
    channels = weight.shape[1]
    return pl.pallas_call(
        back_rest_kernel,
        out_shape=jax.ShapeDtypeStruct((2 * tok, channels), BF16),
        in_specs=[SMEM] + [spec()] * 5,
        out_specs=spec(),
        compiler_params=params(),
        cost_estimate=cost(6 * tok * channels * features, 6 * channels * features),
        name="back_rest",
    )(place, pre, mid, first, second, weight)


def value_kernel(rows_of, scale, dv_ref, *refs):
    slices, out_ref = refs[:-1], refs[-1]
    total, at = None, 0
    for ref, rows in zip(slices, rows_of):
        term = dot_lt(ref[...], dv_ref[at : at + rows, :])
        total = term if total is None else total + term
        at += rows
    out_ref[...] = total * scale


def value_gradient(dv, slices, scale):
    rows_of = tuple(a.shape[0] for a in slices)
    return pl.pallas_call(
        functools.partial(value_kernel, rows_of, scale),
        out_shape=jax.ShapeDtypeStruct((slices[0].shape[1], dv.shape[1]), F32),
        in_specs=[spec()] * (1 + len(slices)),
        out_specs=spec(),
        compiler_params=params(),
        cost_estimate=cost(2 * dv.shape[0] * dv.shape[1] * 192, 2 * dv.size),
        name="value_gradient",
    )(dv, *slices)


def on_device(
    fine_input,
    conv_weight,
    conv_bias,
    norm_gain,
    query_weight,
    key_weight,
    value_weight,
    out_weight,
    cotangent,
):
    samples, fine_rows, channels = fine_input.shape
    tok = fine_rows // 2
    taps, _, features = conv_weight.shape
    n = lax.axis_size("seq")
    grad_scale = 1.0 / math.sqrt(samples * tok * n)
    near = [(i, i ^ 1) for i in range(n)]
    across = [(i, i + 1) for i in range(1, n - 1, 2)] + [(i + 1, i) for i in range(1, n - 1, 2)]
    cycle = list(range(0, n, 2)) + list(range(n - 1, 0, -2))
    ahead = [(cycle[i], cycle[(i + 1) % n]) for i in range(n)]
    behind = [(j, i) for i, j in ahead]
    swap = [(0, 1), (1, 0)]
    place = lax.axis_index("seq").astype(jnp.int32).reshape(1)
    wide = lax.axis_index("wide").astype(jnp.int32).reshape(1)
    bias, gain = conv_bias.reshape(1, features), norm_gain.reshape(1, features)
    fine, cot = fine_input[0], cotangent[0]
    count, core_rows = features // n, tok // 2
    weights = (query_weight, key_weight, value_weight)

    fine_here, edge = edges(fine)
    edge_near, edge_across = lax.ppermute(edge, "seq", near), lax.ppermute(edge, "seq", across)
    att_grad = early(cot, out_weight)
    mine = conv_partial(place, fine_here, edge_near, edge_across, conv_weight)
    theirs = lax.ppermute(mine, "wide", swap)
    normed, message, *weights = norm(wide, mine, theirs, bias, gain, weights, att_grad)
    weights = [near_core(w) for w in weights]

    qkvs, slices = [], []
    cw = ccw = message
    ready = proj = None
    for k in range(1, n // 2 + 1):
        if k > 1:
            cw, ccw, qkvs[-1] = lax.optimization_barrier((cw, ccw, qkvs[-1]))
        if k < n // 2:
            cw, ccw = lax.ppermute(cw, "seq", ahead), lax.ppermute(ccw, "seq", behind)
            blocks = [cw, ccw]
        else:
            blocks = [lax.ppermute(cw, "seq", ahead)]
        sisters = [lax.ppermute(a, "wide", swap) for a in blocks]
        if k == 1:
            qkv, piece, proj = own_project(place, normed, att_grad, *weights, count)
        else:
            qkv, piece = others_project(place, wide, *ready, *weights, count, core_rows)
        qkvs.append(qkv)
        slices.append(piece)
        ready = (blocks, sisters)
    qkv, piece = others_project(place, wide, *ready, *weights, count, core_rows)
    qkvs.append(qkv)
    slices.append(piece)

    both, dv = attention(qkvs, proj, *weights, out_weight, tok)
    there = lax.ppermute(both, "wide", swap)
    value_grad = value_gradient(dv, slices, grad_scale)
    section_out, pre_back, edge, taps_here = finish(
        mine, theirs, bias, gain, cot, both, there, conv_weight
    )
    edge_near, edge_across = lax.ppermute(edge, "seq", near), lax.ppermute(edge, "seq", across)
    taps_here = near_core(taps_here)
    mid = back_mid(pre_back, taps_here)
    input_grad = back_rest(place, pre_back, mid, edge_near, edge_across, taps_here)
    return (section_out[None], input_grad[None], value_grad.T)


def solution(mesh):
    in_specs = (
        P("groups", "seq", "wide"),
        P(None, "wide", None),
        P(),
        P(),
        P(None, "wide"),
        P(None, "wide"),
        P(None, "wide"),
        P("wide", None),
        P("groups", "seq", None),
    )
    out_specs = (P("groups", "seq", None), P("groups", "seq", "wide"), P(("groups", "wide"), "seq"))
    return jax.shard_map(
        on_device, mesh=mesh, in_specs=in_specs, out_specs=out_specs, check_vma=False
    )
```

```python
import functools
import math

import jax
import jax.numpy as jnp
from jax import lax
from jax.experimental import pallas as pl
from jax.experimental.pallas import tpu as pltpu
from jax.sharding import PartitionSpec as P

DH = 192
EPSILON = 1e-06
SCORE_GAIN = 3.0
GELU_ROOT = 0.7978845608028654
GELU_CUBIC = 0.044715
F32 = jnp.float32
BF16 = jnp.bfloat16
HALO_ROWS = 16
CHUNK = 16
SMEM = pl.BlockSpec(memory_space=pltpu.SMEM)
MIB = 1024 * 1024


def spec():
    return pl.BlockSpec(memory_space=pltpu.VMEM)


def in_hbm():
    return pl.BlockSpec(memory_space=pltpu.HBM)


def anywhere():
    return pl.BlockSpec(memory_space=pl.ANY)


def far(value):
    return pltpu.with_memory_space_constraint(value, pltpu.HBM)


def near_core(value):
    return pltpu.with_memory_space_constraint(value, pltpu.VMEM)


def params(limit=8):
    return pltpu.CompilerParams(vmem_limit_bytes=limit * MIB)


def cost(flops, nbytes):
    return pl.CostEstimate(flops=int(flops), bytes_accessed=int(nbytes), transcendentals=0)


def dot(left, right):
    return jnp.dot(left, right, preferred_element_type=F32)


def dot_rt(left, right):
    return lax.dot_general(left, right, (((1,), (1,)), ((), ())), preferred_element_type=F32)


def dot_lt(left, right):
    return lax.dot_general(left, right, (((0,), (0,)), ((), ())), preferred_element_type=F32)


def pick(shape, test):
    row = lax.broadcasted_iota(jnp.int32, shape, 0)
    col = lax.broadcasted_iota(jnp.int32, shape, 1)
    return jnp.where(test(row, col), 1.0, 0.0).astype(BF16)


def edges_kernel(fine_any, fine_ref, edge_ref, sem):
    copy = pltpu.make_async_copy(fine_any, fine_ref, sem)
    copy.start()
    copy.wait()
    rows = fine_ref.shape[0]
    edge_ref[0:2, :] = fine_ref[rows - 2 :, :]
    edge_ref[2:3, :] = fine_ref[0:1, :]


def edges(fine):
    return pl.pallas_call(
        edges_kernel,
        out_shape=[
            jax.ShapeDtypeStruct(fine.shape, BF16),
            jax.ShapeDtypeStruct((3, fine.shape[1]), BF16),
        ],
        in_specs=[in_hbm()],
        out_specs=[spec()] * 2,
        scratch_shapes=[pltpu.SemaphoreType.DMA],
        compiler_params=params(),
        cost_estimate=cost(fine.size, 2 * fine.size),
        name="edges",
    )(far(fine))


def sided(place_ref, first_ref, second_ref, before_rows):
    even = place_ref[0] % 2 == 0
    first, second = first_ref[...].astype(F32), second_ref[...].astype(F32)
    low = lax.broadcasted_iota(jnp.int32, first.shape, 0) < before_rows
    return jnp.where(low == even, second, first).astype(BF16)


def early_kernel(cot_any, wo_any, grad_ref, cot, wo, sems):
    copies = [
        pltpu.make_async_copy(cot_any, cot, sems.at[0]),
        pltpu.make_async_copy(wo_any, wo, sems.at[1]),
    ]
    for c in copies:
        c.start()
    for c in copies:
        c.wait()
    grad_ref[...] = dot_rt(cot[...], wo[...]).astype(BF16)


def early(cot, wo):
    tok, features = cot.shape
    width = wo.shape[0]
    return pl.pallas_call(
        early_kernel,
        out_shape=jax.ShapeDtypeStruct((tok, width), BF16),
        in_specs=[in_hbm()] * 2,
        out_specs=spec(),
        scratch_shapes=[
            pltpu.VMEM((tok, features), BF16),
            pltpu.VMEM(wo.shape, BF16),
            pltpu.SemaphoreType.DMA((2,)),
        ],
        compiler_params=params(),
        cost_estimate=cost(2 * tok * features * width, 2 * wo.size),
        name="early",
    )(far(cot), far(wo))


def conv_kernel(order, fine_ref, taps_any, out_ref, taps, sems):
    fine_rows, channels = fine_ref.shape
    tok = fine_rows // 2
    copies = {k: pltpu.make_async_copy(taps_any.at[k], taps.at[k], sems.at[k]) for k in order}
    for k in order:
        copies[k].start()
    block = fine_ref[...]
    total = None
    for k in order:
        rows = dot(pick((tok, fine_rows), lambda r, c, k=k: c == 2 * r + k - 2), block).astype(BF16)
        copies[k].wait()
        term = dot(rows, taps[k])
        total = term if total is None else total + term
    out_ref[...] = total


def conv_inner(fine, weight):
    taps, channels, features = weight.shape
    tok = fine.shape[0] // 2
    return pl.pallas_call(
        functools.partial(conv_kernel, tuple(range(taps))),
        out_shape=jax.ShapeDtypeStruct((tok, features), F32),
        in_specs=[spec(), in_hbm()],
        out_specs=spec(),
        scratch_shapes=[pltpu.VMEM(weight.shape, BF16), pltpu.SemaphoreType.DMA((taps,))],
        compiler_params=params(12),
        cost_estimate=cost(2 * tok * weight.size, 2 * weight.size),
        name="conv_inner",
    )(fine, far(weight))


def conv_edge_kernel(place_ref, inner_ref, first_ref, second_ref, taps_any, out_ref, taps, sems):
    tok = inner_ref.shape[0]
    copies = [pltpu.make_async_copy(taps_any.at[k], taps.at[i], sems.at[i]) for i, k in enumerate((0, 1, 4))]
    for c in copies:
        c.start()
    side = sided(place_ref, first_ref, second_ref, 2)
    blank = jnp.zeros((CHUNK - 1, side.shape[1]), BF16)
    terms = []
    for i in range(3):
        copies[i].wait()
        terms.append(dot(jnp.concatenate([side[i : i + 1], blank], 0), taps[i])[0:1])
    row = lax.broadcasted_iota(jnp.int32, (CHUNK, 1), 0)
    top = inner_ref[:CHUNK, :] + jnp.where(row == 0, terms[0] + terms[1], 0.0)
    low = inner_ref[tok - CHUNK :, :] + jnp.where(row == CHUNK - 1, terms[2], 0.0)
    out_ref[:CHUNK, :] = top.astype(BF16)
    out_ref[CHUNK : tok - CHUNK, :] = inner_ref[CHUNK : tok - CHUNK, :].astype(BF16)
    out_ref[tok - CHUNK :, :] = low.astype(BF16)


def conv_edge(place, inner, first, second, weight):
    taps, channels, features = weight.shape
    return pl.pallas_call(
        conv_edge_kernel,
        out_shape=jax.ShapeDtypeStruct(inner.shape, BF16),
        in_specs=[SMEM] + [spec()] * 3 + [in_hbm()],
        out_specs=spec(),
        scratch_shapes=[pltpu.VMEM((3, channels, features), BF16), pltpu.SemaphoreType.DMA((3,))],
        compiler_params=params(8),
        cost_estimate=cost(96 * channels * features, 6 * channels * features),
        name="conv_edge",
    )(place, inner, first, second, far(weight))


def gelu_value(preact):
    tangent = jnp.tanh(GELU_ROOT * (preact + GELU_CUBIC * preact * preact * preact))
    return 0.5 * preact * (1.0 + tangent), tangent


def head_scale(value):
    lane = lax.broadcasted_iota(jnp.int32, value.shape, 1)
    square = value * value
    parts = value.shape[1] // DH
    scale = jnp.zeros_like(value)
    for h in range(parts):
        here = (lane >= h * DH) & (lane < (h + 1) * DH)
        mean = jnp.sum(jnp.where(here, square, 0.0), -1, keepdims=True) * (1.0 / DH)
        scale = jnp.where(here, lax.rsqrt(mean + EPSILON), scale)
    return scale


def head_mean(value):
    lane = lax.broadcasted_iota(jnp.int32, value.shape, 1)
    parts = value.shape[1] // DH
    out = jnp.zeros_like(value)
    for h in range(parts):
        here = (lane >= h * DH) & (lane < (h + 1) * DH)
        mean = jnp.sum(jnp.where(here, value, 0.0), -1, keepdims=True) * (1.0 / DH)
        out = jnp.where(here, mean, out)
    return out


def norm_kernel(wide_ref, mine_ref, theirs_ref, bias_ref, gain_ref, *refs):
    weights_any, (grad_ref, normed_ref, message_ref), weights, sems = refs[:3], refs[3:6], refs[6:9], refs[9]
    tok, features = mine_ref.shape
    width = message_ref.shape[1]
    half = tok // 2
    copies = [pltpu.make_async_copy(weights_any[i], weights[i], sems.at[i]) for i in range(3)]
    for c in copies:
        c.start()

    @pl.loop(0, tok // CHUNK)
    def _(i):
        at = pl.ds(pl.multiple_of(i * CHUNK, CHUNK), CHUNK)
        preact = mine_ref[at, :].astype(F32) + theirs_ref[at, :].astype(F32) + bias_ref[...]
        hidden = gelu_value(preact)[0].astype(BF16).astype(F32)
        inv = lax.rsqrt(jnp.mean(hidden * hidden, -1, keepdims=True) + EPSILON)
        normed_ref[at, :] = (hidden * inv * gain_ref[...]).astype(BF16)

    own = normed_ref[pl.ds(pl.multiple_of(wide_ref[0] * half, CHUNK), half), :]
    for j in range(features // width):
        message_ref[j * half : (j + 1) * half, :] = own[:, j * width : (j + 1) * width]
    message_ref[features // width * half :, :] = grad_ref[...]
    for c in copies:
        c.wait()


def norm(wide, mine, theirs, bias, gain, weights, grad):
    tok, features = mine.shape
    width = weights[0].shape[1]
    rows = features // width * (tok // 2) + tok
    return pl.pallas_call(
        norm_kernel,
        out_shape=[
            jax.ShapeDtypeStruct((tok, features), BF16),
            jax.ShapeDtypeStruct((rows, width), BF16),
        ]
        + [pltpu.VMEM(w.shape, BF16) for w in weights],
        in_specs=[SMEM] + [spec()] * 4 + [in_hbm()] * 3 + [spec()],
        out_specs=[spec()] * 5,
        scratch_shapes=[pltpu.SemaphoreType.DMA((3,))],
        compiler_params=params(),
        cost_estimate=cost(30 * tok * features, 6 * tok * features),
        name="norm",
    )(wide, mine, theirs, bias, gain, *[far(w) for w in weights], grad)


def project(value, place_ref, weights, qkv_ref, slice_ref, proj_ref=None):
    features, width = weights[0].shape
    count = slice_ref.shape[1]
    start = place_ref[0] * count
    slice_ref[...] = dot(value, pick((features, count), lambda r, c: r == c + start)).astype(BF16)
    for i, w in enumerate(weights):
        proj = dot(value, w[...])
        if proj_ref is not None and i < 2:
            proj_ref[:, i * width : (i + 1) * width] = proj
        if i < 2:
            proj = proj * head_scale(proj)
        qkv_ref[:, i * width : (i + 1) * width] = proj.astype(BF16)


def own_kernel(place_ref, normed_ref, grad_ref, wq_ref, wk_ref, wv_ref, qkv_ref, slice_ref, proj_ref):
    qkv_ref[:, 3 * wq_ref.shape[1] :] = grad_ref[...]
    project(normed_ref[...], place_ref, (wq_ref, wk_ref, wv_ref), qkv_ref, slice_ref, proj_ref)


def own_project(place, normed, grad, wq, wk, wv, count):
    rows, features = normed.shape
    width = wq.shape[1]
    return pl.pallas_call(
        own_kernel,
        out_shape=[
            jax.ShapeDtypeStruct((rows, 4 * width), BF16),
            jax.ShapeDtypeStruct((rows, count), BF16),
            jax.ShapeDtypeStruct((rows, 2 * width), F32),
        ],
        in_specs=[SMEM] + [spec()] * 5,
        out_specs=[spec()] * 3,
        compiler_params=params(),
        cost_estimate=cost(6 * rows * features * width, 6 * features * width),
        name="own_project",
    )(place, normed, grad, wq, wk, wv)


def others_kernel(count, half, place_ref, wide_ref, *refs):
    mine, theirs = refs[:count], refs[count : 2 * count]
    wq_ref, wk_ref, wv_ref, qkv_ref, slice_ref, lhs = refs[2 * count :]
    width = wq_ref.shape[1]
    for b in range(count):
        for ref, core in ((mine[b], wide_ref[0]), (theirs[b], 1 - wide_ref[0])):
            row = pl.ds(pl.multiple_of(b * 2 * half + core * half, CHUNK), half)
            for j in range(wq_ref.shape[0] // width):
                lhs[row, j * width : (j + 1) * width] = ref[j * half : (j + 1) * half, :]
        base = b * 2 * half
        qkv_ref[base : base + 2 * half, 3 * width :] = mine[b][mine[b].shape[0] - 2 * half :, :]
    project(lhs[...], place_ref, (wq_ref, wk_ref, wv_ref), qkv_ref, slice_ref)


def others_project(place, wide, mine, theirs, wq, wk, wv, count, half):
    features, width = wq.shape
    rows = len(mine) * 2 * half
    return pl.pallas_call(
        functools.partial(others_kernel, len(mine), half),
        out_shape=[
            jax.ShapeDtypeStruct((rows, 4 * width), BF16),
            jax.ShapeDtypeStruct((rows, count), BF16),
        ],
        in_specs=[SMEM] * 2 + [spec()] * (2 * len(mine) + 3),
        out_specs=[spec()] * 2,
        scratch_shapes=[pltpu.VMEM((rows, features), BF16)],
        compiler_params=params(),
        cost_estimate=cost(6 * rows * features * width, 6 * features * width),
        name="others_project",
    )(place, wide, *mine, *theirs, wq, wk, wv)


def attention_kernel(tok, tile, heads, qkv_rows, *refs):
    groups = len(qkv_rows)
    width = heads * DH
    total = sum(qkv_rows)
    qkv_in = refs[:groups]
    proj_ref, wq, wk, wv, wo, both_ref, dv_ref = refs[groups : groups + 7]
    qkv, dv_acc, dk_acc, dq_acc, att, sems = refs[groups + 7 :]
    loads = []
    at = 0
    for i, rows in enumerate(qkv_rows):
        loads.append(pltpu.make_async_copy(qkv_in[i], qkv.at[pl.ds(at, rows)], sems.at[len(loads)]))
        at += rows
    for c in loads:
        c.start()
    for c in loads:
        c.wait()

    scale = SCORE_GAIN / math.sqrt(DH)
    lanes = min(128, tile)

    def block(start, first, h):
        here = pl.ds(start, tile)
        cols = slice(h * DH, (h + 1) * DH)
        key = qkv[:, width + h * DH : width + (h + 1) * DH]
        val = qkv[:, 2 * width + h * DH : 2 * width + (h + 1) * DH]
        query = qkv[here, cols]
        up = qkv[here, 3 * width + h * DH : 3 * width + (h + 1) * DH]
        expo = jnp.exp2(dot_rt(key, query) * (scale * math.log2(math.e)))
        back = dot_rt(val, up)
        inv = 1.0 / jnp.sum(expo, 0, keepdims=True)
        delta = jnp.sum(expo * back, 0, keepdims=True) * inv
        prob_b = (expo * inv).astype(BF16)
        score_own = (expo[:tok] * inv * (back[:tok] - delta) * scale).astype(BF16)
        if first:
            dv_acc[:, cols] = dot(prob_b, up)
            dk_acc[:, cols] = dot(score_own, query)
        else:
            dv_acc[:, cols] += dot(prob_b, up)
            dk_acc[:, cols] += dot(score_own, query)

        def own():
            att[:, cols] = dot_lt(prob_b[:, :lanes], val)[:tok].astype(BF16)
            score = expo[:, :lanes] * inv[:, :lanes] * (back[:, :lanes] - delta[:, :lanes]) * scale
            dq_acc[:, cols] = dot_lt(score.astype(BF16), key)[:tok]

        if first:
            own()
        elif first is None:
            pl.when(start == 0)(own)

    if total <= 2048:
        for step in range(total // tile):
            for h in range(heads):
                block(step * tile, step == 0, h)
    else:
        dv_acc[...] = jnp.zeros_like(dv_acc)
        dk_acc[...] = jnp.zeros_like(dk_acc)
        for h in range(heads):

            @pl.loop(0, total // tile)
            def _(step):
                block(pl.multiple_of(step * tile, tile), None, h)

    dv_ref[...] = dv_acc[...].astype(BF16)
    both_ref[:tok, :] = dot(att[...], wo[...]).astype(BF16)
    backs = []
    for acc, lo in ((dq_acc, 0), (dk_acc, width)):
        proj = proj_ref[:, lo : lo + width]
        inv = head_scale(proj)
        normal = proj * inv
        up = acc[...].astype(BF16).astype(F32)
        backs.append((inv * (up - normal * head_mean(up * normal))).astype(BF16))
    norm_back = dot_rt(backs[0], wq[...]) + dot_rt(backs[1], wk[...]) + dot_rt(dv_ref[:tok, :], wv[...])
    both_ref[tok:, :] = norm_back.astype(BF16)


def attention(qkvs, proj, wq, wk, wv, wo, tok):
    qkv_rows = tuple(a.shape[0] for a in qkvs)
    total = sum(qkv_rows)
    features, width = wq.shape
    heads = width // DH
    tile = 256 if total <= 2048 else 128
    return pl.pallas_call(
        functools.partial(attention_kernel, tok, tile, heads, qkv_rows),
        out_shape=[
            jax.ShapeDtypeStruct((2 * tok, features), BF16),
            jax.ShapeDtypeStruct((total, width), BF16),
        ],
        in_specs=[anywhere()] * len(qkvs) + [spec()] * 5,
        out_specs=[spec()] * 2,
        scratch_shapes=[
            pltpu.VMEM((total, 4 * width), BF16),
            pltpu.VMEM((total, width), F32),
            pltpu.VMEM((tok, width), F32),
            pltpu.VMEM((tok, width), F32),
            pltpu.VMEM((tok, width), BF16),
            pltpu.SemaphoreType.DMA((len(qkvs),)),
        ],
        compiler_params=params(24 if total <= 2048 else 56),
        cost_estimate=cost(6 * total * total * width, 8 * total * width),
        name="attention",
    )(*qkvs, proj, wq, wk, wv, wo)


def local_kernel(mine_ref, theirs_ref, bias_ref, hidden_ref, slope_ref):
    @pl.loop(0, mine_ref.shape[0] // CHUNK)
    def _(i):
        at = pl.ds(pl.multiple_of(i * CHUNK, CHUNK), CHUNK)
        preact = mine_ref[at, :].astype(F32) + theirs_ref[at, :].astype(F32) + bias_ref[...]
        active, tangent = gelu_value(preact)
        hidden_ref[at, :] = active.astype(BF16)
        slope_ref[at, :] = 0.5 * (1.0 + tangent) + 0.5 * preact * (1.0 - tangent * tangent) * GELU_ROOT * (
            1.0 + 3.0 * GELU_CUBIC * preact * preact
        )


def local_terms(mine, theirs, bias):
    return pl.pallas_call(
        local_kernel,
        out_shape=[jax.ShapeDtypeStruct(mine.shape, BF16), jax.ShapeDtypeStruct(mine.shape, F32)],
        in_specs=[spec()] * 3,
        out_specs=[spec()] * 2,
        compiler_params=params(),
        cost_estimate=cost(40 * mine.size, 10 * mine.size),
        name="local_terms",
    )(mine, theirs, bias)


def finish_kernel(hidden_ref, slope_ref, gain_ref, cot_ref, here_ref, there_ref, *refs):
    taps_any, out_ref, pre_ref, edge_ref, taps_ref, sem = refs
    tok = out_ref.shape[0]
    copy = pltpu.make_async_copy(taps_any.at[pl.ds(2, 2)], taps_ref, sem)
    copy.start()

    @pl.loop(0, tok // CHUNK)
    def _(i):
        at = pl.ds(pl.multiple_of(i * CHUNK, CHUNK), CHUNK)
        low = pl.ds(pl.multiple_of(tok + i * CHUNK, CHUNK), CHUNK)
        hidden = hidden_ref[at, :].astype(F32)
        inv = lax.rsqrt(jnp.mean(hidden * hidden, -1, keepdims=True) + EPSILON)
        out_ref[at, :] = (hidden + (here_ref[at, :].astype(F32) + there_ref[at, :].astype(F32))).astype(BF16)
        gain_back = (here_ref[low, :].astype(F32) + there_ref[low, :].astype(F32)) * gain_ref[...]
        mean = jnp.mean(gain_back * hidden, -1, keepdims=True)
        back = cot_ref[at, :].astype(F32) + inv * (gain_back - hidden * (inv * inv * mean))
        pre_ref[at, :] = (back * slope_ref[at, :]).astype(BF16)

    edge_ref[0:1, :] = pre_ref[tok - 1 : tok, :]
    edge_ref[1:2, :] = pre_ref[0:1, :]
    copy.wait()


def finish(hidden, slope, gain, cot, here, there, taps):
    tok, features = cot.shape
    row = jax.ShapeDtypeStruct((2, features), BF16)
    full = jax.ShapeDtypeStruct((tok, features), BF16)
    return pl.pallas_call(
        finish_kernel,
        out_shape=[full, full, row, pltpu.VMEM((2,) + taps.shape[1:], BF16)],
        in_specs=[spec()] * 6 + [in_hbm()],
        out_specs=[spec()] * 4,
        scratch_shapes=[pltpu.SemaphoreType.DMA],
        compiler_params=params(16),
        cost_estimate=cost(40 * tok * features, 12 * tok * features),
        name="finish",
    )(hidden, slope, gain, cot, here, there, far(taps))


def back_mid_kernel(pre_ref, weight_ref, taps_any, out_ref, taps_ref, sems):
    channels = weight_ref.shape[1]
    copies = [pltpu.make_async_copy(taps_any.at[k], taps_ref.at[i], sems.at[i]) for i, k in enumerate((0, 1, 4))]
    for c in copies:
        c.start()
    pre = pre_ref[...]
    out_ref[:, :channels] = dot_rt(pre, weight_ref[0])
    out_ref[:, channels:] = dot_rt(pre, weight_ref[1])
    for c in copies:
        c.wait()


def back_mid(pre, weight, taps):
    tok, features = pre.shape
    channels = weight.shape[1]
    return pl.pallas_call(
        back_mid_kernel,
        out_shape=[
            jax.ShapeDtypeStruct((tok, 2 * channels), F32),
            pltpu.VMEM((3,) + taps.shape[1:], BF16),
        ],
        in_specs=[spec()] * 2 + [in_hbm()],
        out_specs=[spec()] * 2,
        scratch_shapes=[pltpu.SemaphoreType.DMA((3,))],
        compiler_params=params(),
        cost_estimate=cost(4 * tok * channels * features, 10 * channels * features),
        name="back_mid",
    )(pre, weight, far(taps))


def back_rest_kernel(place_ref, pre_ref, mid_ref, first_ref, second_ref, weight_ref, out_ref):
    tok, channels = pre_ref.shape[0], weight_ref.shape[1]
    pre = pre_ref[...]
    side = sided(place_ref, first_ref, second_ref, 1)
    after = jnp.concatenate([pre[1:], side[1:2]], 0)
    before = jnp.concatenate([side[0:1], pre[:-1]], 0)
    first = mid_ref[:, :channels] + dot_rt(after, weight_ref[0]) + dot_rt(before, weight_ref[2])
    second = mid_ref[:, channels:] + dot_rt(after, weight_ref[1])
    even = pick((2 * tok, tok), lambda r, c: r == 2 * c)
    odd = pick((2 * tok, tok), lambda r, c: r == 2 * c + 1)
    out_ref[...] = (dot(even, first.astype(BF16)) + dot(odd, second.astype(BF16))).astype(BF16)


def back_rest(place, pre, mid, first, second, weight):
    tok, features = pre.shape
    channels = weight.shape[1]
    return pl.pallas_call(
        back_rest_kernel,
        out_shape=jax.ShapeDtypeStruct((2 * tok, channels), BF16),
        in_specs=[SMEM] + [spec()] * 5,
        out_specs=spec(),
        compiler_params=params(),
        cost_estimate=cost(6 * tok * channels * features, 6 * channels * features),
        name="back_rest",
    )(place, pre, mid, first, second, weight)


def value_kernel(rows_of, scale, dv_ref, *refs):
    slices, out_ref = refs[:-1], refs[-1]
    total, at = None, 0
    for ref, rows in zip(slices, rows_of):
        term = dot_lt(ref[...], dv_ref[at : at + rows, :])
        total = term if total is None else total + term
        at += rows
    out_ref[...] = total * scale


def value_gradient(dv, slices, scale):
    rows_of = tuple(a.shape[0] for a in slices)
    return pl.pallas_call(
        functools.partial(value_kernel, rows_of, scale),
        out_shape=jax.ShapeDtypeStruct((slices[0].shape[1], dv.shape[1]), F32),
        in_specs=[spec()] * (1 + len(slices)),
        out_specs=spec(),
        compiler_params=params(),
        cost_estimate=cost(2 * dv.shape[0] * dv.shape[1] * 192, 2 * dv.size),
        name="value_gradient",
    )(dv, *slices)


def on_device(
    fine_input,
    conv_weight,
    conv_bias,
    norm_gain,
    query_weight,
    key_weight,
    value_weight,
    out_weight,
    cotangent,
):
    samples, fine_rows, channels = fine_input.shape
    tok = fine_rows // 2
    taps, _, features = conv_weight.shape
    n = lax.axis_size("seq")
    grad_scale = 1.0 / math.sqrt(samples * tok * n)
    near = [(i, i ^ 1) for i in range(n)]
    across = [(i, i + 1) for i in range(1, n - 1, 2)] + [(i + 1, i) for i in range(1, n - 1, 2)]
    cycle = list(range(0, n, 2)) + list(range(n - 1, 0, -2))
    ahead = [(cycle[i], cycle[(i + 1) % n]) for i in range(n)]
    behind = [(j, i) for i, j in ahead]
    swap = [(0, 1), (1, 0)]
    place = lax.axis_index("seq").astype(jnp.int32).reshape(1)
    wide = lax.axis_index("wide").astype(jnp.int32).reshape(1)
    bias, gain = conv_bias.reshape(1, features), norm_gain.reshape(1, features)
    fine, cot = fine_input[0], cotangent[0]
    count, core_rows = features // n, tok // 2
    weights = (query_weight, key_weight, value_weight)

    fine_here, edge = edges(fine)
    edge_near, edge_across = lax.ppermute(edge, "seq", near), lax.ppermute(edge, "seq", across)
    att_grad = early(cot, out_weight)
    inner = conv_inner(fine_here, conv_weight)
    mine = conv_edge(place, inner, edge_near, edge_across, conv_weight)
    theirs = lax.ppermute(mine, "wide", swap)
    normed, message, *weights = norm(wide, mine, theirs, bias, gain, weights, att_grad)
    weights = [near_core(w) for w in weights]

    local = local_terms(mine, theirs, bias)
    qkvs, slices = [], []
    cw = ccw = message
    ready = proj = None
    for k in range(1, n // 2 + 1):
        if k == 2:
            cw, ccw, qkvs[0] = lax.optimization_barrier((cw, ccw, qkvs[0]))
        elif k == 3:
            cw, ccw, local = lax.optimization_barrier((cw, ccw, local))
        elif k > 3:
            cw, ccw, qkvs[k - 3], qkvs[k - 2] = lax.optimization_barrier(
                (cw, ccw, qkvs[k - 3], qkvs[k - 2])
            )
        if k < n // 2:
            cw, ccw = lax.ppermute(cw, "seq", ahead), lax.ppermute(ccw, "seq", behind)
            blocks = [cw, ccw]
        else:
            blocks = [lax.ppermute(cw, "seq", ahead)]
        sisters = [lax.ppermute(a, "wide", swap) for a in blocks]
        if k == 1:
            qkv, piece, proj = own_project(place, normed, att_grad, *weights, count)
        else:
            qkv, piece = others_project(place, wide, *ready, *weights, count, core_rows)
        qkvs.append(qkv)
        slices.append(piece)
        ready = (blocks, sisters)
    qkv, piece = others_project(place, wide, *ready, *weights, count, core_rows)
    qkvs.append(qkv)
    slices.append(piece)

    both, dv = attention(qkvs, proj, *weights, out_weight, tok)
    there = lax.ppermute(both, "wide", swap)
    value_grad = value_gradient(dv, slices, grad_scale)
    section_out, pre_back, edge, taps_here = finish(
        *local, gain, cot, both, there, conv_weight
    )
    edge_near, edge_across = lax.ppermute(edge, "seq", near), lax.ppermute(edge, "seq", across)
    taps_here = near_core(taps_here)
    mid, taps_side = back_mid(pre_back, taps_here, conv_weight)
    taps_side = near_core(taps_side)
    input_grad = back_rest(place, pre_back, mid, edge_near, edge_across, taps_side)
    return (section_out[None], input_grad[None], value_grad.T)


def solution(mesh):
    in_specs = (
        P("groups", "seq", "wide"),
        P(None, "wide", None),
        P(),
        P(),
        P(None, "wide"),
        P(None, "wide"),
        P(None, "wide"),
        P("wide", None),
        P("groups", "seq", None),
    )
    out_specs = (P("groups", "seq", None), P("groups", "seq", "wide"), P(("groups", "wide"), "seq"))
    return jax.shard_map(
        on_device, mesh=mesh, in_specs=in_specs, out_specs=out_specs, check_vma=False
    )
```

```python
import functools
import math

import jax
import jax.numpy as jnp
from jax import lax
from jax.experimental import pallas as pl
from jax.experimental.pallas import tpu as pltpu
from jax.sharding import PartitionSpec as P

DH = 192
EPSILON = 1e-06
SCORE_GAIN = 3.0
GELU_ROOT = 0.7978845608028654
GELU_CUBIC = 0.044715
F32 = jnp.float32
BF16 = jnp.bfloat16
HALO_ROWS = 16
CHUNK = 16
SMEM = pl.BlockSpec(memory_space=pltpu.SMEM)
MIB = 1024 * 1024


def spec():
    return pl.BlockSpec(memory_space=pltpu.VMEM)


def in_hbm():
    return pl.BlockSpec(memory_space=pltpu.HBM)


def anywhere():
    return pl.BlockSpec(memory_space=pl.ANY)


def far(value):
    return pltpu.with_memory_space_constraint(value, pltpu.HBM)


def near_core(value):
    return pltpu.with_memory_space_constraint(value, pltpu.VMEM)


def params(limit=8):
    return pltpu.CompilerParams(vmem_limit_bytes=limit * MIB)


def cost(flops, nbytes):
    return pl.CostEstimate(flops=int(flops), bytes_accessed=int(nbytes), transcendentals=0)


def dot(left, right):
    return jnp.dot(left, right, preferred_element_type=F32)


def dot_rt(left, right):
    return lax.dot_general(left, right, (((1,), (1,)), ((), ())), preferred_element_type=F32)


def dot_lt(left, right):
    return lax.dot_general(left, right, (((0,), (0,)), ((), ())), preferred_element_type=F32)


def pick(shape, test):
    row = lax.broadcasted_iota(jnp.int32, shape, 0)
    col = lax.broadcasted_iota(jnp.int32, shape, 1)
    return jnp.where(test(row, col), 1.0, 0.0).astype(BF16)


def edges_kernel(fine_any, fine_ref, edge_ref, sem):
    copy = pltpu.make_async_copy(fine_any, fine_ref, sem)
    copy.start()
    copy.wait()
    rows = fine_ref.shape[0]
    edge_ref[0:2, :] = fine_ref[rows - 2 :, :]
    edge_ref[2:3, :] = fine_ref[0:1, :]


def edges(fine):
    return pl.pallas_call(
        edges_kernel,
        out_shape=[
            jax.ShapeDtypeStruct(fine.shape, BF16),
            jax.ShapeDtypeStruct((3, fine.shape[1]), BF16),
        ],
        in_specs=[in_hbm()],
        out_specs=[spec()] * 2,
        scratch_shapes=[pltpu.SemaphoreType.DMA],
        compiler_params=params(),
        cost_estimate=cost(fine.size, 2 * fine.size),
        name="edges",
    )(far(fine))


def sided(place_ref, first_ref, second_ref, before_rows):
    even = place_ref[0] % 2 == 0
    first, second = first_ref[...].astype(F32), second_ref[...].astype(F32)
    low = lax.broadcasted_iota(jnp.int32, first.shape, 0) < before_rows
    return jnp.where(low == even, second, first).astype(BF16)


def early_kernel(cot_any, wo_any, grad_ref, cot, wo, sems):
    copies = [
        pltpu.make_async_copy(cot_any, cot, sems.at[0]),
        pltpu.make_async_copy(wo_any, wo, sems.at[1]),
    ]
    for c in copies:
        c.start()
    for c in copies:
        c.wait()
    grad_ref[...] = dot_rt(cot[...], wo[...]).astype(BF16)


def early(cot, wo):
    tok, features = cot.shape
    width = wo.shape[0]
    return pl.pallas_call(
        early_kernel,
        out_shape=jax.ShapeDtypeStruct((tok, width), BF16),
        in_specs=[in_hbm()] * 2,
        out_specs=spec(),
        scratch_shapes=[
            pltpu.VMEM((tok, features), BF16),
            pltpu.VMEM(wo.shape, BF16),
            pltpu.SemaphoreType.DMA((2,)),
        ],
        compiler_params=params(),
        cost_estimate=cost(2 * tok * features * width, 2 * wo.size),
        name="early",
    )(far(cot), far(wo))


def conv_kernel(order, fine_ref, taps_any, out_ref, taps, sems):
    fine_rows, channels = fine_ref.shape
    tok = fine_rows // 2
    copies = {k: pltpu.make_async_copy(taps_any.at[k], taps.at[k], sems.at[k]) for k in order}
    for k in order:
        copies[k].start()
    block = fine_ref[...]
    total = None
    for k in order:
        rows = dot(pick((tok, fine_rows), lambda r, c, k=k: c == 2 * r + k - 2), block).astype(BF16)
        copies[k].wait()
        term = dot(rows, taps[k])
        total = term if total is None else total + term
    out_ref[...] = total


def conv_inner(fine, weight):
    taps, channels, features = weight.shape
    tok = fine.shape[0] // 2
    return pl.pallas_call(
        functools.partial(conv_kernel, tuple(range(taps))),
        out_shape=jax.ShapeDtypeStruct((tok, features), F32),
        in_specs=[spec(), in_hbm()],
        out_specs=spec(),
        scratch_shapes=[pltpu.VMEM(weight.shape, BF16), pltpu.SemaphoreType.DMA((taps,))],
        compiler_params=params(12),
        cost_estimate=cost(2 * tok * weight.size, 2 * weight.size),
        name="conv_inner",
    )(fine, far(weight))


def conv_edge_kernel(place_ref, inner_ref, first_ref, second_ref, taps_any, out_ref, taps, sems):
    tok = inner_ref.shape[0]
    copies = [pltpu.make_async_copy(taps_any.at[k], taps.at[i], sems.at[i]) for i, k in enumerate((0, 1, 4))]
    for c in copies:
        c.start()
    side = sided(place_ref, first_ref, second_ref, 2)
    blank = jnp.zeros((CHUNK - 1, side.shape[1]), BF16)
    terms = []
    for i in range(3):
        copies[i].wait()
        terms.append(dot(jnp.concatenate([side[i : i + 1], blank], 0), taps[i])[0:1])
    row = lax.broadcasted_iota(jnp.int32, (CHUNK, 1), 0)
    top = inner_ref[:CHUNK, :] + jnp.where(row == 0, terms[0] + terms[1], 0.0)
    low = inner_ref[tok - CHUNK :, :] + jnp.where(row == CHUNK - 1, terms[2], 0.0)
    out_ref[:CHUNK, :] = top.astype(BF16)
    out_ref[CHUNK : tok - CHUNK, :] = inner_ref[CHUNK : tok - CHUNK, :].astype(BF16)
    out_ref[tok - CHUNK :, :] = low.astype(BF16)


def conv_edge(place, inner, first, second, weight):
    taps, channels, features = weight.shape
    return pl.pallas_call(
        conv_edge_kernel,
        out_shape=jax.ShapeDtypeStruct(inner.shape, BF16),
        in_specs=[SMEM] + [spec()] * 3 + [in_hbm()],
        out_specs=spec(),
        scratch_shapes=[pltpu.VMEM((3, channels, features), BF16), pltpu.SemaphoreType.DMA((3,))],
        compiler_params=params(8),
        cost_estimate=cost(96 * channels * features, 6 * channels * features),
        name="conv_edge",
    )(place, inner, first, second, far(weight))


def gelu_value(preact):
    tangent = jnp.tanh(GELU_ROOT * (preact + GELU_CUBIC * preact * preact * preact))
    return 0.5 * preact * (1.0 + tangent), tangent


def head_scale(value):
    lane = lax.broadcasted_iota(jnp.int32, value.shape, 1)
    square = value * value
    parts = value.shape[1] // DH
    scale = jnp.zeros_like(value)
    for h in range(parts):
        here = (lane >= h * DH) & (lane < (h + 1) * DH)
        mean = jnp.sum(jnp.where(here, square, 0.0), -1, keepdims=True) * (1.0 / DH)
        scale = jnp.where(here, lax.rsqrt(mean + EPSILON), scale)
    return scale


def head_mean(value):
    lane = lax.broadcasted_iota(jnp.int32, value.shape, 1)
    parts = value.shape[1] // DH
    out = jnp.zeros_like(value)
    for h in range(parts):
        here = (lane >= h * DH) & (lane < (h + 1) * DH)
        mean = jnp.sum(jnp.where(here, value, 0.0), -1, keepdims=True) * (1.0 / DH)
        out = jnp.where(here, mean, out)
    return out


def norm_kernel(wide_ref, mine_ref, theirs_ref, bias_ref, gain_ref, *refs):
    weights_any, (grad_ref, normed_ref, message_ref), weights, sems = refs[:3], refs[3:6], refs[6:9], refs[9]
    tok, features = mine_ref.shape
    width = message_ref.shape[1]
    half = tok // 2
    copies = [pltpu.make_async_copy(weights_any[i], weights[i], sems.at[i]) for i in range(3)]
    for c in copies:
        c.start()

    @pl.loop(0, tok // CHUNK)
    def _(i):
        at = pl.ds(pl.multiple_of(i * CHUNK, CHUNK), CHUNK)
        preact = mine_ref[at, :].astype(F32) + theirs_ref[at, :].astype(F32) + bias_ref[...]
        hidden = gelu_value(preact)[0].astype(BF16).astype(F32)
        inv = lax.rsqrt(jnp.mean(hidden * hidden, -1, keepdims=True) + EPSILON)
        normed_ref[at, :] = (hidden * inv * gain_ref[...]).astype(BF16)

    own = normed_ref[pl.ds(pl.multiple_of(wide_ref[0] * half, CHUNK), half), :]
    for j in range(features // width):
        message_ref[j * half : (j + 1) * half, :] = own[:, j * width : (j + 1) * width]
    message_ref[features // width * half :, :] = grad_ref[...]
    for c in copies:
        c.wait()


def norm(wide, mine, theirs, bias, gain, weights, grad):
    tok, features = mine.shape
    width = weights[0].shape[1]
    rows = features // width * (tok // 2) + tok
    return pl.pallas_call(
        norm_kernel,
        out_shape=[
            jax.ShapeDtypeStruct((tok, features), BF16),
            jax.ShapeDtypeStruct((rows, width), BF16),
        ]
        + [pltpu.VMEM(w.shape, BF16) for w in weights],
        in_specs=[SMEM] + [spec()] * 4 + [in_hbm()] * 3 + [spec()],
        out_specs=[spec()] * 5,
        scratch_shapes=[pltpu.SemaphoreType.DMA((3,))],
        compiler_params=params(),
        cost_estimate=cost(30 * tok * features, 6 * tok * features),
        name="norm",
    )(wide, mine, theirs, bias, gain, *[far(w) for w in weights], grad)


def project(value, chosen, weights, qkv_ref, slice_ref, proj_ref=None):
    width = weights[0].shape[1]
    slice_ref[...] = dot(value, chosen).astype(BF16)
    for i, w in enumerate(weights):
        proj = dot(value, w[...])
        if proj_ref is not None and i < 2:
            proj_ref[:, i * width : (i + 1) * width] = proj
        if i < 2:
            proj = proj * head_scale(proj)
        qkv_ref[:, i * width : (i + 1) * width] = proj.astype(BF16)


def own_kernel(place_ref, normed_ref, grad_ref, wq_ref, wk_ref, wv_ref, qkv_ref, slice_ref, proj_ref, chosen_ref):
    count = slice_ref.shape[1]
    start = place_ref[0] * count
    chosen_ref[...] = pick(chosen_ref.shape, lambda r, c: r == c + start)
    qkv_ref[:, 3 * wq_ref.shape[1] :] = grad_ref[...]
    project(normed_ref[...], chosen_ref[...], (wq_ref, wk_ref, wv_ref), qkv_ref, slice_ref, proj_ref)


def own_project(place, normed, grad, wq, wk, wv, count):
    rows, features = normed.shape
    width = wq.shape[1]
    return pl.pallas_call(
        own_kernel,
        out_shape=[
            jax.ShapeDtypeStruct((rows, 4 * width), BF16),
            jax.ShapeDtypeStruct((rows, count), BF16),
            jax.ShapeDtypeStruct((rows, 2 * width), F32),
            jax.ShapeDtypeStruct((features, count), BF16),
        ],
        in_specs=[SMEM] + [spec()] * 5,
        out_specs=[spec()] * 4,
        compiler_params=params(),
        cost_estimate=cost(6 * rows * features * width, 6 * features * width),
        name="own_project",
    )(place, normed, grad, wq, wk, wv)


def others_kernel(count, half, wide_ref, chosen_ref, *refs):
    mine, theirs = refs[:count], refs[count : 2 * count]
    wq_ref, wk_ref, wv_ref, qkv_ref, slice_ref, lhs = refs[2 * count :]
    width = wq_ref.shape[1]
    for b in range(count):
        for ref, core in ((mine[b], wide_ref[0]), (theirs[b], 1 - wide_ref[0])):
            row = pl.ds(pl.multiple_of(b * 2 * half + core * half, CHUNK), half)
            for j in range(wq_ref.shape[0] // width):
                lhs[row, j * width : (j + 1) * width] = ref[j * half : (j + 1) * half, :]
        base = b * 2 * half
        qkv_ref[base : base + 2 * half, 3 * width :] = mine[b][mine[b].shape[0] - 2 * half :, :]
    project(lhs[...], chosen_ref[...], (wq_ref, wk_ref, wv_ref), qkv_ref, slice_ref)


def others_project(wide, chosen, mine, theirs, wq, wk, wv, count, half):
    features, width = wq.shape
    rows = len(mine) * 2 * half
    return pl.pallas_call(
        functools.partial(others_kernel, len(mine), half),
        out_shape=[
            jax.ShapeDtypeStruct((rows, 4 * width), BF16),
            jax.ShapeDtypeStruct((rows, count), BF16),
        ],
        in_specs=[SMEM] + [spec()] * (2 * len(mine) + 4),
        out_specs=[spec()] * 2,
        scratch_shapes=[pltpu.VMEM((rows, features), BF16)],
        compiler_params=params(),
        cost_estimate=cost(6 * rows * features * width, 6 * features * width),
        name="others_project",
    )(wide, chosen, *mine, *theirs, wq, wk, wv)


def attention_kernel(tok, tile, heads, qkv_rows, *refs):
    groups = len(qkv_rows)
    width = heads * DH
    total = sum(qkv_rows)
    qkv_in = refs[:groups]
    proj_ref, wq, wk, wv, wo, both_ref, dv_ref = refs[groups : groups + 7]
    qkv, dv_acc, dk_acc, dq_acc, att, sems = refs[groups + 7 :]
    at, loads = 0, []
    for i, rows in enumerate(qkv_rows):
        if total <= 1024:
            qkv[at : at + rows, :] = qkv_in[i][...]
        else:
            loads.append(pltpu.make_async_copy(qkv_in[i], qkv.at[pl.ds(at, rows)], sems.at[i]))
        at += rows
    for c in loads:
        c.start()
    for c in loads:
        c.wait()

    scale = SCORE_GAIN / math.sqrt(DH)
    lanes = min(128, tile)

    def block(start, first, h):
        here = pl.ds(start, tile)
        cols = slice(h * DH, (h + 1) * DH)
        key = qkv[:, width + h * DH : width + (h + 1) * DH]
        val = qkv[:, 2 * width + h * DH : 2 * width + (h + 1) * DH]
        query = qkv[here, cols]
        up = qkv[here, 3 * width + h * DH : 3 * width + (h + 1) * DH]
        expo = jnp.exp2(dot_rt(key, query) * (scale * math.log2(math.e)))
        back = dot_rt(val, up)
        inv = 1.0 / jnp.sum(expo, 0, keepdims=True)
        delta = jnp.sum(expo * back, 0, keepdims=True) * inv
        prob_b = (expo * inv).astype(BF16)
        score_own = (expo[:tok] * inv * (back[:tok] - delta) * scale).astype(BF16)
        if first:
            dv_acc[:, cols] = dot(prob_b, up)
            dk_acc[:, cols] = dot(score_own, query)
        else:
            dv_acc[:, cols] += dot(prob_b, up)
            dk_acc[:, cols] += dot(score_own, query)

        def own():
            att[:, cols] = dot_lt(prob_b[:, :lanes], val)[:tok].astype(BF16)
            score = expo[:, :lanes] * inv[:, :lanes] * (back[:, :lanes] - delta[:, :lanes]) * scale
            dq_acc[:, cols] = dot_lt(score.astype(BF16), key)[:tok]

        if first:
            own()
        elif first is None:
            pl.when(start == 0)(own)

    if total <= 1024:
        for step in range(total // tile):
            for h in range(heads):
                block(step * tile, step == 0, h)
    else:
        dv_acc[...] = jnp.zeros_like(dv_acc)
        dk_acc[...] = jnp.zeros_like(dk_acc)
        for h in range(heads):

            @pl.loop(0, total // tile)
            def _(step):
                block(pl.multiple_of(step * tile, tile), None, h)

    dv_ref[...] = dv_acc[...].astype(BF16)
    both_ref[:tok, :] = dot(att[...], wo[...]).astype(BF16)
    backs = []
    for acc, lo in ((dq_acc, 0), (dk_acc, width)):
        proj = proj_ref[:, lo : lo + width]
        inv = head_scale(proj)
        normal = proj * inv
        up = acc[...].astype(BF16).astype(F32)
        backs.append((inv * (up - normal * head_mean(up * normal))).astype(BF16))
    norm_back = dot_rt(backs[0], wq[...]) + dot_rt(backs[1], wk[...]) + dot_rt(dv_ref[:tok, :], wv[...])
    both_ref[tok:, :] = norm_back.astype(BF16)


def attention(qkvs, proj, wq, wk, wv, wo, tok):
    qkv_rows = tuple(a.shape[0] for a in qkvs)
    total = sum(qkv_rows)
    features, width = wq.shape
    heads = width // DH
    tile = total if total <= 1024 else 128
    return pl.pallas_call(
        functools.partial(attention_kernel, tok, tile, heads, qkv_rows),
        out_shape=[
            jax.ShapeDtypeStruct((2 * tok, features), BF16),
            jax.ShapeDtypeStruct((total, width), BF16),
        ],
        in_specs=[spec() if total <= 1024 else anywhere()] * len(qkvs) + [spec()] * 5,
        out_specs=[spec()] * 2,
        scratch_shapes=[
            pltpu.VMEM((total, 4 * width), BF16),
            pltpu.VMEM((total, width), F32),
            pltpu.VMEM((tok, width), F32),
            pltpu.VMEM((tok, width), F32),
            pltpu.VMEM((tok, width), BF16),
            pltpu.SemaphoreType.DMA((len(qkvs),)),
        ],
        compiler_params=params(32 if total <= 1024 else 56),
        cost_estimate=cost(6 * total * total * width, 8 * total * width),
        name="attention",
    )(*qkvs, proj, wq, wk, wv, wo)


def local_kernel(mine_ref, theirs_ref, bias_ref, hidden_ref, slope_ref):
    @pl.loop(0, mine_ref.shape[0] // CHUNK)
    def _(i):
        at = pl.ds(pl.multiple_of(i * CHUNK, CHUNK), CHUNK)
        preact = mine_ref[at, :].astype(F32) + theirs_ref[at, :].astype(F32) + bias_ref[...]
        active, tangent = gelu_value(preact)
        hidden_ref[at, :] = active.astype(BF16)
        slope_ref[at, :] = 0.5 * (1.0 + tangent) + 0.5 * preact * (1.0 - tangent * tangent) * GELU_ROOT * (
            1.0 + 3.0 * GELU_CUBIC * preact * preact
        )


def local_terms(mine, theirs, bias):
    return pl.pallas_call(
        local_kernel,
        out_shape=[jax.ShapeDtypeStruct(mine.shape, BF16), jax.ShapeDtypeStruct(mine.shape, F32)],
        in_specs=[spec()] * 3,
        out_specs=[spec()] * 2,
        compiler_params=params(),
        cost_estimate=cost(40 * mine.size, 10 * mine.size),
        name="local_terms",
    )(mine, theirs, bias)


def finish_kernel(hidden_ref, slope_ref, gain_ref, cot_ref, here_ref, there_ref, *refs):
    taps_any, out_ref, pre_ref, edge_ref, taps_ref, sem = refs
    tok = out_ref.shape[0]
    copy = pltpu.make_async_copy(taps_any.at[pl.ds(2, 2)], taps_ref, sem)
    copy.start()

    @pl.loop(0, tok // CHUNK)
    def _(i):
        at = pl.ds(pl.multiple_of(i * CHUNK, CHUNK), CHUNK)
        low = pl.ds(pl.multiple_of(tok + i * CHUNK, CHUNK), CHUNK)
        hidden = hidden_ref[at, :].astype(F32)
        inv = lax.rsqrt(jnp.mean(hidden * hidden, -1, keepdims=True) + EPSILON)
        out_ref[at, :] = (hidden + (here_ref[at, :].astype(F32) + there_ref[at, :].astype(F32))).astype(BF16)
        gain_back = (here_ref[low, :].astype(F32) + there_ref[low, :].astype(F32)) * gain_ref[...]
        mean = jnp.mean(gain_back * hidden, -1, keepdims=True)
        back = cot_ref[at, :].astype(F32) + inv * (gain_back - hidden * (inv * inv * mean))
        pre_ref[at, :] = (back * slope_ref[at, :]).astype(BF16)

    edge_ref[0:1, :] = pre_ref[tok - 1 : tok, :]
    edge_ref[1:2, :] = pre_ref[0:1, :]
    copy.wait()


def finish(hidden, slope, gain, cot, here, there, taps):
    tok, features = cot.shape
    row = jax.ShapeDtypeStruct((2, features), BF16)
    full = jax.ShapeDtypeStruct((tok, features), BF16)
    return pl.pallas_call(
        finish_kernel,
        out_shape=[full, full, row, pltpu.VMEM((2,) + taps.shape[1:], BF16)],
        in_specs=[spec()] * 6 + [in_hbm()],
        out_specs=[spec()] * 4,
        scratch_shapes=[pltpu.SemaphoreType.DMA],
        compiler_params=params(16),
        cost_estimate=cost(40 * tok * features, 12 * tok * features),
        name="finish",
    )(hidden, slope, gain, cot, here, there, far(taps))


def back_mid_kernel(pre_ref, weight_ref, taps_any, out_ref, taps_ref, sems):
    channels = weight_ref.shape[1]
    copies = [pltpu.make_async_copy(taps_any.at[k], taps_ref.at[i], sems.at[i]) for i, k in enumerate((0, 1, 4))]
    for c in copies:
        c.start()
    pre = pre_ref[...]
    out_ref[:, :channels] = dot_rt(pre, weight_ref[0])
    out_ref[:, channels:] = dot_rt(pre, weight_ref[1])
    for c in copies:
        c.wait()


def back_mid(pre, weight, taps):
    tok, features = pre.shape
    channels = weight.shape[1]
    return pl.pallas_call(
        back_mid_kernel,
        out_shape=[
            jax.ShapeDtypeStruct((tok, 2 * channels), F32),
            pltpu.VMEM((3,) + taps.shape[1:], BF16),
        ],
        in_specs=[spec()] * 2 + [in_hbm()],
        out_specs=[spec()] * 2,
        scratch_shapes=[pltpu.SemaphoreType.DMA((3,))],
        compiler_params=params(),
        cost_estimate=cost(4 * tok * channels * features, 10 * channels * features),
        name="back_mid",
    )(pre, weight, far(taps))


def back_rest_kernel(place_ref, pre_ref, mid_ref, first_ref, second_ref, weight_ref, out_ref):
    tok, channels = pre_ref.shape[0], weight_ref.shape[1]
    pre = pre_ref[...]
    side = sided(place_ref, first_ref, second_ref, 1)
    after = jnp.concatenate([pre[1:], side[1:2]], 0)
    before = jnp.concatenate([side[0:1], pre[:-1]], 0)
    first = mid_ref[:, :channels] + dot_rt(after, weight_ref[0]) + dot_rt(before, weight_ref[2])
    second = mid_ref[:, channels:] + dot_rt(after, weight_ref[1])
    even = pick((2 * tok, tok), lambda r, c: r == 2 * c)
    odd = pick((2 * tok, tok), lambda r, c: r == 2 * c + 1)
    out_ref[...] = (dot(even, first.astype(BF16)) + dot(odd, second.astype(BF16))).astype(BF16)


def back_rest(place, pre, mid, first, second, weight):
    tok, features = pre.shape
    channels = weight.shape[1]
    return pl.pallas_call(
        back_rest_kernel,
        out_shape=jax.ShapeDtypeStruct((2 * tok, channels), BF16),
        in_specs=[SMEM] + [spec()] * 5,
        out_specs=spec(),
        compiler_params=params(),
        cost_estimate=cost(6 * tok * channels * features, 6 * channels * features),
        name="back_rest",
    )(place, pre, mid, first, second, weight)


def value_kernel(rows_of, scale, dv_ref, *refs):
    slices, out_ref = refs[:-1], refs[-1]
    total, at = None, 0
    for ref, rows in zip(slices, rows_of):
        term = dot_lt(ref[...], dv_ref[at : at + rows, :])
        total = term if total is None else total + term
        at += rows
    out_ref[...] = total * scale


def value_gradient(dv, slices, scale):
    rows_of = tuple(a.shape[0] for a in slices)
    return pl.pallas_call(
        functools.partial(value_kernel, rows_of, scale),
        out_shape=jax.ShapeDtypeStruct((slices[0].shape[1], dv.shape[1]), F32),
        in_specs=[spec()] * (1 + len(slices)),
        out_specs=spec(),
        compiler_params=params(),
        cost_estimate=cost(2 * dv.shape[0] * dv.shape[1] * 192, 2 * dv.size),
        name="value_gradient",
    )(dv, *slices)


def on_device(
    fine_input,
    conv_weight,
    conv_bias,
    norm_gain,
    query_weight,
    key_weight,
    value_weight,
    out_weight,
    cotangent,
):
    samples, fine_rows, channels = fine_input.shape
    tok = fine_rows // 2
    taps, _, features = conv_weight.shape
    n = lax.axis_size("seq")
    grad_scale = 1.0 / math.sqrt(samples * tok * n)
    near = [(i, i ^ 1) for i in range(n)]
    across = [(i, i + 1) for i in range(1, n - 1, 2)] + [(i + 1, i) for i in range(1, n - 1, 2)]
    cycle = list(range(0, n, 2)) + list(range(n - 1, 0, -2))
    ahead = [(cycle[i], cycle[(i + 1) % n]) for i in range(n)]
    behind = [(j, i) for i, j in ahead]
    swap = [(0, 1), (1, 0)]
    place = lax.axis_index("seq").astype(jnp.int32).reshape(1)
    wide = lax.axis_index("wide").astype(jnp.int32).reshape(1)
    bias, gain = conv_bias.reshape(1, features), norm_gain.reshape(1, features)
    fine, cot = fine_input[0], cotangent[0]
    count, core_rows = features // n, tok // 2
    weights = (query_weight, key_weight, value_weight)

    fine_here, edge = edges(fine)
    edge_near, edge_across = lax.ppermute(edge, "seq", near), lax.ppermute(edge, "seq", across)
    att_grad = early(cot, out_weight)
    inner = conv_inner(fine_here, conv_weight)
    mine = conv_edge(place, inner, edge_near, edge_across, conv_weight)
    theirs = lax.ppermute(mine, "wide", swap)
    normed, message, *weights = norm(wide, mine, theirs, bias, gain, weights, att_grad)
    weights = [near_core(w) for w in weights]

    local = local_terms(mine, theirs, bias)
    qkvs, slices = [], []
    cw = ccw = message
    ready = proj = None
    for k in range(1, n // 2 + 1):
        if k == 2:
            cw, ccw, qkvs[0] = lax.optimization_barrier((cw, ccw, qkvs[0]))
        elif k == 3:
            cw, ccw, local = lax.optimization_barrier((cw, ccw, local))
        elif k > 3:
            cw, ccw, qkvs[k - 3], qkvs[k - 2] = lax.optimization_barrier(
                (cw, ccw, qkvs[k - 3], qkvs[k - 2])
            )
        if k < n // 2:
            cw, ccw = lax.ppermute(cw, "seq", ahead), lax.ppermute(ccw, "seq", behind)
            blocks = [cw, ccw]
        else:
            blocks = [lax.ppermute(cw, "seq", ahead)]
        sisters = [lax.ppermute(a, "wide", swap) for a in blocks]
        if k == 1:
            qkv, piece, proj, chosen = own_project(place, normed, att_grad, *weights, count)
        else:
            qkv, piece = others_project(wide, chosen, *ready, *weights, count, core_rows)
        qkvs.append(qkv)
        slices.append(piece)
        ready = (blocks, sisters)
    qkv, piece = others_project(wide, chosen, *ready, *weights, count, core_rows)
    qkvs.append(qkv)
    slices.append(piece)

    both, dv = attention(qkvs, proj, *weights, out_weight, tok)
    there = lax.ppermute(both, "wide", swap)
    value_grad = value_gradient(dv, slices, grad_scale)
    section_out, pre_back, edge, taps_here = finish(
        *local, gain, cot, both, there, conv_weight
    )
    edge_near, edge_across = lax.ppermute(edge, "seq", near), lax.ppermute(edge, "seq", across)
    taps_here = near_core(taps_here)
    mid, taps_side = back_mid(pre_back, taps_here, conv_weight)
    taps_side = near_core(taps_side)
    input_grad = back_rest(place, pre_back, mid, edge_near, edge_across, taps_side)
    return (section_out[None], input_grad[None], value_grad.T)


def solution(mesh):
    in_specs = (
        P("groups", "seq", "wide"),
        P(None, "wide", None),
        P(),
        P(),
        P(None, "wide"),
        P(None, "wide"),
        P(None, "wide"),
        P("wide", None),
        P("groups", "seq", None),
    )
    out_specs = (P("groups", "seq", None), P("groups", "seq", "wide"), P(("groups", "wide"), "seq"))
    return jax.shard_map(
        on_device, mesh=mesh, in_specs=in_specs, out_specs=out_specs, check_vma=False
    )
```

```python
import functools
import math

import jax
import jax.numpy as jnp
from jax import lax
from jax.experimental import pallas as pl
from jax.experimental.pallas import tpu as pltpu
from jax.sharding import PartitionSpec as P

DH = 192
EPSILON = 1e-06
SCORE_GAIN = 3.0
GELU_ROOT = 0.7978845608028654
GELU_CUBIC = 0.044715
F32 = jnp.float32
BF16 = jnp.bfloat16
HALO_ROWS = 16
CHUNK = 16
SMEM = pl.BlockSpec(memory_space=pltpu.SMEM)
MIB = 1024 * 1024


def spec():
    return pl.BlockSpec(memory_space=pltpu.VMEM)


def in_hbm():
    return pl.BlockSpec(memory_space=pltpu.HBM)


def anywhere():
    return pl.BlockSpec(memory_space=pl.ANY)


def far(value):
    return pltpu.with_memory_space_constraint(value, pltpu.HBM)


def near_core(value):
    return pltpu.with_memory_space_constraint(value, pltpu.VMEM)


def params(limit=8):
    return pltpu.CompilerParams(vmem_limit_bytes=limit * MIB)


def cost(flops, nbytes):
    return pl.CostEstimate(flops=int(flops), bytes_accessed=int(nbytes), transcendentals=0)


def dot(left, right):
    return jnp.dot(left, right, preferred_element_type=F32)


def dot_rt(left, right):
    return lax.dot_general(left, right, (((1,), (1,)), ((), ())), preferred_element_type=F32)


def dot_lt(left, right):
    return lax.dot_general(left, right, (((0,), (0,)), ((), ())), preferred_element_type=F32)


def pick(shape, test):
    row = lax.broadcasted_iota(jnp.int32, shape, 0)
    col = lax.broadcasted_iota(jnp.int32, shape, 1)
    return jnp.where(test(row, col), 1.0, 0.0).astype(BF16)


def edges_kernel(fine_any, edge_ref, top, low, sems):
    rows = fine_any.shape[0]
    copies = [
        pltpu.make_async_copy(fine_any.at[pl.ds(0, CHUNK)], top, sems.at[0]),
        pltpu.make_async_copy(fine_any.at[pl.ds(rows - CHUNK, CHUNK)], low, sems.at[1]),
    ]
    for c in copies:
        c.start()
    for c in copies:
        c.wait()
    edge_ref[0:2, :] = low[CHUNK - 2 :, :]
    edge_ref[2:3, :] = top[0:1, :]


def edges(fine):
    channels = fine.shape[1]
    return pl.pallas_call(
        edges_kernel,
        out_shape=jax.ShapeDtypeStruct((3, channels), BF16),
        in_specs=[in_hbm()],
        out_specs=spec(),
        scratch_shapes=[
            pltpu.VMEM((CHUNK, channels), BF16),
            pltpu.VMEM((CHUNK, channels), BF16),
            pltpu.SemaphoreType.DMA((2,)),
        ],
        compiler_params=params(),
        cost_estimate=cost(channels, 64 * channels),
        name="edges",
    )(far(fine))


def sided(place_ref, first_ref, second_ref, before_rows):
    even = place_ref[0] % 2 == 0
    first, second = first_ref[...].astype(F32), second_ref[...].astype(F32)
    low = lax.broadcasted_iota(jnp.int32, first.shape, 0) < before_rows
    return jnp.where(low == even, second, first).astype(BF16)


def early_kernel(cot_any, wo_any, grad_ref, cot, wo, sems):
    copies = [
        pltpu.make_async_copy(cot_any, cot, sems.at[0]),
        pltpu.make_async_copy(wo_any, wo, sems.at[1]),
    ]
    for c in copies:
        c.start()
    for c in copies:
        c.wait()
    grad_ref[...] = dot_rt(cot[...], wo[...]).astype(BF16)


def early(cot, wo):
    tok, features = cot.shape
    width = wo.shape[0]
    return pl.pallas_call(
        early_kernel,
        out_shape=jax.ShapeDtypeStruct((tok, width), BF16),
        in_specs=[in_hbm()] * 2,
        out_specs=spec(),
        scratch_shapes=[
            pltpu.VMEM((tok, features), BF16),
            pltpu.VMEM(wo.shape, BF16),
            pltpu.SemaphoreType.DMA((2,)),
        ],
        compiler_params=params(),
        cost_estimate=cost(2 * tok * features * width, 2 * wo.size),
        name="early",
    )(far(cot), far(wo))


def conv_kernel(order, fine_any, taps_any, out_ref, fine, taps, sems):
    fine_rows, channels = fine.shape
    fine_copy = pltpu.make_async_copy(fine_any, fine, sems.at[len(order)])
    fine_copy.start()
    tok = fine_rows // 2
    copies = {k: pltpu.make_async_copy(taps_any.at[k], taps.at[k], sems.at[k]) for k in order}
    for k in order:
        copies[k].start()
    fine_copy.wait()
    block = fine[...]
    total = None
    for k in order:
        rows = dot(pick((tok, fine_rows), lambda r, c, k=k: c == 2 * r + k - 2), block).astype(BF16)
        copies[k].wait()
        term = dot(rows, taps[k])
        total = term if total is None else total + term
    out_ref[...] = total


def conv_inner(fine, weight):
    taps, channels, features = weight.shape
    tok = fine.shape[0] // 2
    return pl.pallas_call(
        functools.partial(conv_kernel, tuple(range(taps))),
        out_shape=jax.ShapeDtypeStruct((tok, features), F32),
        in_specs=[in_hbm()] * 2,
        out_specs=spec(),
        scratch_shapes=[
            pltpu.VMEM(fine.shape, BF16),
            pltpu.VMEM(weight.shape, BF16),
            pltpu.SemaphoreType.DMA((taps + 1,)),
        ],
        compiler_params=params(12),
        cost_estimate=cost(2 * tok * weight.size, 2 * weight.size),
        name="conv_inner",
    )(far(fine), far(weight))


def conv_edge_kernel(place_ref, inner_ref, first_ref, second_ref, taps_any, out_ref, taps, sems):
    tok = inner_ref.shape[0]
    copies = [pltpu.make_async_copy(taps_any.at[k], taps.at[i], sems.at[i]) for i, k in enumerate((0, 1, 4))]
    for c in copies:
        c.start()
    side = sided(place_ref, first_ref, second_ref, 2)
    blank = jnp.zeros((CHUNK - 1, side.shape[1]), BF16)
    terms = []
    for i in range(3):
        copies[i].wait()
        terms.append(dot(jnp.concatenate([side[i : i + 1], blank], 0), taps[i])[0:1])
    row = lax.broadcasted_iota(jnp.int32, (CHUNK, 1), 0)
    top = inner_ref[:CHUNK, :] + jnp.where(row == 0, terms[0] + terms[1], 0.0)
    low = inner_ref[tok - CHUNK :, :] + jnp.where(row == CHUNK - 1, terms[2], 0.0)
    out_ref[:CHUNK, :] = top.astype(BF16)
    out_ref[CHUNK : tok - CHUNK, :] = inner_ref[CHUNK : tok - CHUNK, :].astype(BF16)
    out_ref[tok - CHUNK :, :] = low.astype(BF16)


def conv_edge(place, inner, first, second, weight):
    taps, channels, features = weight.shape
    return pl.pallas_call(
        conv_edge_kernel,
        out_shape=jax.ShapeDtypeStruct(inner.shape, BF16),
        in_specs=[SMEM] + [spec()] * 3 + [in_hbm()],
        out_specs=spec(),
        scratch_shapes=[pltpu.VMEM((3, channels, features), BF16), pltpu.SemaphoreType.DMA((3,))],
        compiler_params=params(8),
        cost_estimate=cost(96 * channels * features, 6 * channels * features),
        name="conv_edge",
    )(place, inner, first, second, far(weight))


def gelu_value(preact):
    tangent = jnp.tanh(GELU_ROOT * (preact + GELU_CUBIC * preact * preact * preact))
    return 0.5 * preact * (1.0 + tangent), tangent


def head_scale(value):
    lane = lax.broadcasted_iota(jnp.int32, value.shape, 1)
    square = value * value
    parts = value.shape[1] // DH
    scale = jnp.zeros_like(value)
    for h in range(parts):
        here = (lane >= h * DH) & (lane < (h + 1) * DH)
        mean = jnp.sum(jnp.where(here, square, 0.0), -1, keepdims=True) * (1.0 / DH)
        scale = jnp.where(here, lax.rsqrt(mean + EPSILON), scale)
    return scale


def head_mean(value):
    lane = lax.broadcasted_iota(jnp.int32, value.shape, 1)
    parts = value.shape[1] // DH
    out = jnp.zeros_like(value)
    for h in range(parts):
        here = (lane >= h * DH) & (lane < (h + 1) * DH)
        mean = jnp.sum(jnp.where(here, value, 0.0), -1, keepdims=True) * (1.0 / DH)
        out = jnp.where(here, mean, out)
    return out


def norm_kernel(wide_ref, mine_ref, theirs_ref, bias_ref, gain_ref, *refs):
    weights_any, (grad_ref, normed_ref, message_ref), weights, sems = refs[:3], refs[3:6], refs[6:9], refs[9]
    tok, features = mine_ref.shape
    width = message_ref.shape[1]
    half = tok // 2
    copies = [pltpu.make_async_copy(weights_any[i], weights[i], sems.at[i]) for i in range(3)]
    for c in copies:
        c.start()

    @pl.loop(0, tok // CHUNK)
    def _(i):
        at = pl.ds(pl.multiple_of(i * CHUNK, CHUNK), CHUNK)
        preact = mine_ref[at, :].astype(F32) + theirs_ref[at, :].astype(F32) + bias_ref[...]
        hidden = gelu_value(preact)[0].astype(BF16).astype(F32)
        inv = lax.rsqrt(jnp.mean(hidden * hidden, -1, keepdims=True) + EPSILON)
        normed_ref[at, :] = (hidden * inv * gain_ref[...]).astype(BF16)

    own = normed_ref[pl.ds(pl.multiple_of(wide_ref[0] * half, CHUNK), half), :]
    for j in range(features // width):
        message_ref[j * half : (j + 1) * half, :] = own[:, j * width : (j + 1) * width]
    message_ref[features // width * half :, :] = grad_ref[...]
    for c in copies:
        c.wait()


def norm(wide, mine, theirs, bias, gain, weights, grad):
    tok, features = mine.shape
    width = weights[0].shape[1]
    rows = features // width * (tok // 2) + tok
    return pl.pallas_call(
        norm_kernel,
        out_shape=[
            jax.ShapeDtypeStruct((tok, features), BF16),
            jax.ShapeDtypeStruct((rows, width), BF16),
        ]
        + [pltpu.VMEM(w.shape, BF16) for w in weights],
        in_specs=[SMEM] + [spec()] * 4 + [in_hbm()] * 3 + [spec()],
        out_specs=[spec()] * 5,
        scratch_shapes=[pltpu.SemaphoreType.DMA((3,))],
        compiler_params=params(),
        cost_estimate=cost(30 * tok * features, 6 * tok * features),
        name="norm",
    )(wide, mine, theirs, bias, gain, *[far(w) for w in weights], grad)


def project(value, chosen, weights, qkv_ref, slice_ref, proj_ref=None):
    width = weights[0].shape[1]
    slice_ref[...] = dot(value, chosen).astype(BF16)
    for i, w in enumerate(weights):
        proj = dot(value, w[...])
        if proj_ref is not None and i < 2:
            proj_ref[:, i * width : (i + 1) * width] = proj
        if i < 2:
            proj = proj * head_scale(proj)
        qkv_ref[:, i * width : (i + 1) * width] = proj.astype(BF16)


def own_kernel(place_ref, normed_ref, grad_ref, wq_ref, wk_ref, wv_ref, qkv_ref, slice_ref, proj_ref, chosen_ref):
    count = slice_ref.shape[1]
    start = place_ref[0] * count
    chosen_ref[...] = pick(chosen_ref.shape, lambda r, c: r == c + start)
    qkv_ref[:, 3 * wq_ref.shape[1] :] = grad_ref[...]
    project(normed_ref[...], chosen_ref[...], (wq_ref, wk_ref, wv_ref), qkv_ref, slice_ref, proj_ref)


def own_project(place, normed, grad, wq, wk, wv, count):
    rows, features = normed.shape
    width = wq.shape[1]
    return pl.pallas_call(
        own_kernel,
        out_shape=[
            jax.ShapeDtypeStruct((rows, 4 * width), BF16),
            jax.ShapeDtypeStruct((rows, count), BF16),
            jax.ShapeDtypeStruct((rows, 2 * width), F32),
            jax.ShapeDtypeStruct((features, count), BF16),
        ],
        in_specs=[SMEM] + [spec()] * 5,
        out_specs=[spec()] * 4,
        compiler_params=params(),
        cost_estimate=cost(6 * rows * features * width, 6 * features * width),
        name="own_project",
    )(place, normed, grad, wq, wk, wv)


def others_kernel(count, half, wide_ref, chosen_ref, *refs):
    mine, theirs = refs[:count], refs[count : 2 * count]
    wq_ref, wk_ref, wv_ref, qkv_ref, slice_ref, lhs = refs[2 * count :]
    width = wq_ref.shape[1]
    for b in range(count):
        for ref, core in ((mine[b], wide_ref[0]), (theirs[b], 1 - wide_ref[0])):
            row = pl.ds(pl.multiple_of(b * 2 * half + core * half, CHUNK), half)
            for j in range(wq_ref.shape[0] // width):
                lhs[row, j * width : (j + 1) * width] = ref[j * half : (j + 1) * half, :]
        base = b * 2 * half
        qkv_ref[base : base + 2 * half, 3 * width :] = mine[b][mine[b].shape[0] - 2 * half :, :]
    project(lhs[...], chosen_ref[...], (wq_ref, wk_ref, wv_ref), qkv_ref, slice_ref)


def others_project(wide, chosen, mine, theirs, wq, wk, wv, count, half):
    features, width = wq.shape
    rows = len(mine) * 2 * half
    return pl.pallas_call(
        functools.partial(others_kernel, len(mine), half),
        out_shape=[
            jax.ShapeDtypeStruct((rows, 4 * width), BF16),
            jax.ShapeDtypeStruct((rows, count), BF16),
        ],
        in_specs=[SMEM] + [spec()] * (2 * len(mine) + 4),
        out_specs=[spec()] * 2,
        scratch_shapes=[pltpu.VMEM((rows, features), BF16)],
        compiler_params=params(),
        cost_estimate=cost(6 * rows * features * width, 6 * features * width),
        name="others_project",
    )(wide, chosen, *mine, *theirs, wq, wk, wv)


def attention_kernel(tok, tile, heads, qkv_rows, *refs):
    groups = len(qkv_rows)
    width = heads * DH
    total = sum(qkv_rows)
    qkv_in = refs[:groups]
    proj_ref, wq, wk, wv, wo, both_ref, dv_ref = refs[groups : groups + 7]
    qkv, dv_acc, dk_acc, dq_acc, att, sems = refs[groups + 7 :]
    at, loads = 0, []
    for i, rows in enumerate(qkv_rows):
        if total <= 1024:
            qkv[at : at + rows, :] = qkv_in[i][...]
        else:
            loads.append(pltpu.make_async_copy(qkv_in[i], qkv.at[pl.ds(at, rows)], sems.at[i]))
        at += rows
    for c in loads:
        c.start()
    for c in loads:
        c.wait()

    scale = SCORE_GAIN / math.sqrt(DH)
    lanes = min(128, tile)

    def block(start, first, h):
        here = pl.ds(start, tile)
        cols = slice(h * DH, (h + 1) * DH)
        key = qkv[:, width + h * DH : width + (h + 1) * DH]
        val = qkv[:, 2 * width + h * DH : 2 * width + (h + 1) * DH]
        query = qkv[here, cols]
        up = qkv[here, 3 * width + h * DH : 3 * width + (h + 1) * DH]
        expo = jnp.exp2(dot_rt(key, query) * (scale * math.log2(math.e)))
        back = dot_rt(val, up)
        inv = 1.0 / jnp.sum(expo, 0, keepdims=True)
        delta = jnp.sum(expo * back, 0, keepdims=True) * inv
        prob_b = (expo * inv).astype(BF16)
        score_own = (expo[:tok] * inv * (back[:tok] - delta) * scale).astype(BF16)
        if tile == total:
            dv_ref[:, cols] = dot(prob_b, up).astype(BF16)
            dk_acc[:, cols] = dot(score_own, query)
        elif first:
            dv_acc[:, cols] = dot(prob_b, up)
            dk_acc[:, cols] = dot(score_own, query)
        else:
            dv_acc[:, cols] += dot(prob_b, up)
            dk_acc[:, cols] += dot(score_own, query)

        def own():
            att[:, cols] = dot_lt(prob_b[:, :lanes], val)[:tok].astype(BF16)
            score = expo[:, :lanes] * inv[:, :lanes] * (back[:, :lanes] - delta[:, :lanes]) * scale
            dq_acc[:, cols] = dot_lt(score.astype(BF16), key)[:tok]

        if first:
            own()
        elif first is None:
            pl.when(start == 0)(own)

    if total <= 1024:
        for step in range(total // tile):
            for h in range(heads):
                block(step * tile, step == 0, h)
    else:
        dv_acc[...] = jnp.zeros_like(dv_acc)
        dk_acc[...] = jnp.zeros_like(dk_acc)
        for h in range(heads):

            @pl.loop(0, total // tile)
            def _(step):
                block(pl.multiple_of(step * tile, tile), None, h)

    if tile != total:
        dv_ref[...] = dv_acc[...].astype(BF16)
    both_ref[:tok, :] = dot(att[...], wo[...]).astype(BF16)
    backs = []
    for acc, lo in ((dq_acc, 0), (dk_acc, width)):
        proj = proj_ref[:, lo : lo + width]
        inv = head_scale(proj)
        normal = proj * inv
        up = acc[...].astype(BF16).astype(F32)
        backs.append((inv * (up - normal * head_mean(up * normal))).astype(BF16))
    norm_back = dot_rt(backs[0], wq[...]) + dot_rt(backs[1], wk[...]) + dot_rt(dv_ref[:tok, :], wv[...])
    both_ref[tok:, :] = norm_back.astype(BF16)


def attention(qkvs, proj, wq, wk, wv, wo, tok):
    qkv_rows = tuple(a.shape[0] for a in qkvs)
    total = sum(qkv_rows)
    features, width = wq.shape
    heads = width // DH
    tile = total if total <= 1024 else 128
    return pl.pallas_call(
        functools.partial(attention_kernel, tok, tile, heads, qkv_rows),
        out_shape=[
            jax.ShapeDtypeStruct((2 * tok, features), BF16),
            jax.ShapeDtypeStruct((total, width), BF16),
        ],
        in_specs=[spec() if total <= 1024 else anywhere()] * len(qkvs) + [spec()] * 5,
        out_specs=[spec()] * 2,
        scratch_shapes=[
            pltpu.VMEM((total, 4 * width), BF16),
            pltpu.VMEM((total, width), F32),
            pltpu.VMEM((tok, width), F32),
            pltpu.VMEM((tok, width), F32),
            pltpu.VMEM((tok, width), BF16),
            pltpu.SemaphoreType.DMA((len(qkvs),)),
        ],
        compiler_params=params(32 if total <= 1024 else 56),
        cost_estimate=cost(6 * total * total * width, 8 * total * width),
        name="attention",
    )(*qkvs, proj, wq, wk, wv, wo)


def local_kernel(mine_ref, theirs_ref, bias_ref, hidden_ref, slope_ref):
    @pl.loop(0, mine_ref.shape[0] // CHUNK)
    def _(i):
        at = pl.ds(pl.multiple_of(i * CHUNK, CHUNK), CHUNK)
        preact = mine_ref[at, :].astype(F32) + theirs_ref[at, :].astype(F32) + bias_ref[...]
        active, tangent = gelu_value(preact)
        hidden_ref[at, :] = active.astype(BF16)
        slope_ref[at, :] = 0.5 * (1.0 + tangent) + 0.5 * preact * (1.0 - tangent * tangent) * GELU_ROOT * (
            1.0 + 3.0 * GELU_CUBIC * preact * preact
        )


def local_terms(mine, theirs, bias):
    return pl.pallas_call(
        local_kernel,
        out_shape=[jax.ShapeDtypeStruct(mine.shape, BF16), jax.ShapeDtypeStruct(mine.shape, F32)],
        in_specs=[spec()] * 3,
        out_specs=[spec()] * 2,
        compiler_params=params(),
        cost_estimate=cost(40 * mine.size, 10 * mine.size),
        name="local_terms",
    )(mine, theirs, bias)


def finish_kernel(hidden_ref, slope_ref, gain_ref, cot_ref, here_ref, there_ref, *refs):
    taps_any, out_ref, pre_ref, edge_ref, taps_ref, sem = refs
    tok = out_ref.shape[0]
    copy = pltpu.make_async_copy(taps_any.at[pl.ds(2, 2)], taps_ref, sem)
    copy.start()

    @pl.loop(0, tok // CHUNK)
    def _(i):
        at = pl.ds(pl.multiple_of(i * CHUNK, CHUNK), CHUNK)
        low = pl.ds(pl.multiple_of(tok + i * CHUNK, CHUNK), CHUNK)
        hidden = hidden_ref[at, :].astype(F32)
        inv = lax.rsqrt(jnp.mean(hidden * hidden, -1, keepdims=True) + EPSILON)
        out_ref[at, :] = (hidden + (here_ref[at, :].astype(F32) + there_ref[at, :].astype(F32))).astype(BF16)
        gain_back = (here_ref[low, :].astype(F32) + there_ref[low, :].astype(F32)) * gain_ref[...]
        mean = jnp.mean(gain_back * hidden, -1, keepdims=True)
        back = cot_ref[at, :].astype(F32) + inv * (gain_back - hidden * (inv * inv * mean))
        pre_ref[at, :] = (back * slope_ref[at, :]).astype(BF16)

    edge_ref[0:1, :] = pre_ref[tok - 1 : tok, :]
    edge_ref[1:2, :] = pre_ref[0:1, :]
    copy.wait()


def finish(hidden, slope, gain, cot, here, there, taps):
    tok, features = cot.shape
    row = jax.ShapeDtypeStruct((2, features), BF16)
    full = jax.ShapeDtypeStruct((tok, features), BF16)
    return pl.pallas_call(
        finish_kernel,
        out_shape=[full, full, row, pltpu.VMEM((2,) + taps.shape[1:], BF16)],
        in_specs=[spec()] * 6 + [in_hbm()],
        out_specs=[spec()] * 4,
        scratch_shapes=[pltpu.SemaphoreType.DMA],
        compiler_params=params(16),
        cost_estimate=cost(40 * tok * features, 12 * tok * features),
        name="finish",
    )(hidden, slope, gain, cot, here, there, far(taps))


def back_mid_kernel(pre_ref, weight_ref, taps_any, out_ref, taps_ref, sems):
    channels = weight_ref.shape[1]
    copies = [pltpu.make_async_copy(taps_any.at[k], taps_ref.at[i], sems.at[i]) for i, k in enumerate((0, 1, 4))]
    for c in copies:
        c.start()
    pre = pre_ref[...]
    out_ref[:, :channels] = dot_rt(pre, weight_ref[0])
    out_ref[:, channels:] = dot_rt(pre, weight_ref[1])
    for c in copies:
        c.wait()


def back_mid(pre, weight, taps):
    tok, features = pre.shape
    channels = weight.shape[1]
    return pl.pallas_call(
        back_mid_kernel,
        out_shape=[
            jax.ShapeDtypeStruct((tok, 2 * channels), F32),
            pltpu.VMEM((3,) + taps.shape[1:], BF16),
        ],
        in_specs=[spec()] * 2 + [in_hbm()],
        out_specs=[spec()] * 2,
        scratch_shapes=[pltpu.SemaphoreType.DMA((3,))],
        compiler_params=params(),
        cost_estimate=cost(4 * tok * channels * features, 10 * channels * features),
        name="back_mid",
    )(pre, weight, far(taps))


def back_rest_kernel(place_ref, pre_ref, mid_ref, first_ref, second_ref, weight_ref, out_ref):
    tok, channels = pre_ref.shape[0], weight_ref.shape[1]
    pre = pre_ref[...]
    side = sided(place_ref, first_ref, second_ref, 1)
    after = jnp.concatenate([pre[1:], side[1:2]], 0)
    before = jnp.concatenate([side[0:1], pre[:-1]], 0)
    first = mid_ref[:, :channels] + dot_rt(after, weight_ref[0]) + dot_rt(before, weight_ref[2])
    second = mid_ref[:, channels:] + dot_rt(after, weight_ref[1])
    even = pick((2 * tok, tok), lambda r, c: r == 2 * c)
    odd = pick((2 * tok, tok), lambda r, c: r == 2 * c + 1)
    out_ref[...] = (dot(even, first.astype(BF16)) + dot(odd, second.astype(BF16))).astype(BF16)


def back_rest(place, pre, mid, first, second, weight):
    tok, features = pre.shape
    channels = weight.shape[1]
    return pl.pallas_call(
        back_rest_kernel,
        out_shape=jax.ShapeDtypeStruct((2 * tok, channels), BF16),
        in_specs=[SMEM] + [spec()] * 5,
        out_specs=spec(),
        compiler_params=params(),
        cost_estimate=cost(6 * tok * channels * features, 6 * channels * features),
        name="back_rest",
    )(place, pre, mid, first, second, weight)


def value_kernel(rows_of, scale, dv_ref, *refs):
    slices, out_ref = refs[:-1], refs[-1]
    total, at = None, 0
    for ref, rows in zip(slices, rows_of):
        term = dot_lt(ref[...], dv_ref[at : at + rows, :])
        total = term if total is None else total + term
        at += rows
    out_ref[...] = total * scale


def value_gradient(dv, slices, scale):
    rows_of = tuple(a.shape[0] for a in slices)
    return pl.pallas_call(
        functools.partial(value_kernel, rows_of, scale),
        out_shape=jax.ShapeDtypeStruct((slices[0].shape[1], dv.shape[1]), F32),
        in_specs=[spec()] * (1 + len(slices)),
        out_specs=spec(),
        compiler_params=params(),
        cost_estimate=cost(2 * dv.shape[0] * dv.shape[1] * 192, 2 * dv.size),
        name="value_gradient",
    )(dv, *slices)


def on_device(
    fine_input,
    conv_weight,
    conv_bias,
    norm_gain,
    query_weight,
    key_weight,
    value_weight,
    out_weight,
    cotangent,
):
    samples, fine_rows, channels = fine_input.shape
    tok = fine_rows // 2
    taps, _, features = conv_weight.shape
    n = lax.axis_size("seq")
    grad_scale = 1.0 / math.sqrt(samples * tok * n)
    near = [(i, i ^ 1) for i in range(n)]
    across = [(i, i + 1) for i in range(1, n - 1, 2)] + [(i + 1, i) for i in range(1, n - 1, 2)]
    cycle = list(range(0, n, 2)) + list(range(n - 1, 0, -2))
    ahead = [(cycle[i], cycle[(i + 1) % n]) for i in range(n)]
    behind = [(j, i) for i, j in ahead]
    swap = [(0, 1), (1, 0)]
    place = lax.axis_index("seq").astype(jnp.int32).reshape(1)
    wide = lax.axis_index("wide").astype(jnp.int32).reshape(1)
    bias, gain = conv_bias.reshape(1, features), norm_gain.reshape(1, features)
    fine, cot = fine_input[0], cotangent[0]
    count, core_rows = features // n, tok // 2
    weights = (query_weight, key_weight, value_weight)

    edge = edges(fine)
    edge_near, edge_across = lax.ppermute(edge, "seq", near), lax.ppermute(edge, "seq", across)
    att_grad = early(cot, out_weight)
    inner = conv_inner(fine, conv_weight)
    mine = conv_edge(place, inner, edge_near, edge_across, conv_weight)
    theirs = lax.ppermute(mine, "wide", swap)
    normed, message, *weights = norm(wide, mine, theirs, bias, gain, weights, att_grad)
    weights = [near_core(w) for w in weights]

    local = local_terms(mine, theirs, bias)
    qkvs, slices = [], []
    cw = ccw = message
    ready = proj = None
    for k in range(1, n // 2 + 1):
        if k == 2:
            cw, ccw, qkvs[0] = lax.optimization_barrier((cw, ccw, qkvs[0]))
        elif k == 3:
            cw, ccw, local = lax.optimization_barrier((cw, ccw, local))
        elif k > 3:
            cw, ccw, qkvs[k - 3], qkvs[k - 2] = lax.optimization_barrier(
                (cw, ccw, qkvs[k - 3], qkvs[k - 2])
            )
        if k < n // 2:
            cw, ccw = lax.ppermute(cw, "seq", ahead), lax.ppermute(ccw, "seq", behind)
            blocks = [cw, ccw]
        else:
            blocks = [lax.ppermute(cw, "seq", ahead)]
        sisters = [lax.ppermute(a, "wide", swap) for a in blocks]
        if k == 1:
            qkv, piece, proj, chosen = own_project(place, normed, att_grad, *weights, count)
        else:
            qkv, piece = others_project(wide, chosen, *ready, *weights, count, core_rows)
        qkvs.append(qkv)
        slices.append(piece)
        ready = (blocks, sisters)
    qkv, piece = others_project(wide, chosen, *ready, *weights, count, core_rows)
    qkvs.append(qkv)
    slices.append(piece)

    both, dv = attention(qkvs, proj, *weights, out_weight, tok)
    there = lax.ppermute(both, "wide", swap)
    value_grad = value_gradient(dv, slices, grad_scale)
    section_out, pre_back, edge, taps_here = finish(
        *local, gain, cot, both, there, conv_weight
    )
    edge_near, edge_across = lax.ppermute(edge, "seq", near), lax.ppermute(edge, "seq", across)
    taps_here = near_core(taps_here)
    mid, taps_side = back_mid(pre_back, taps_here, conv_weight)
    taps_side = near_core(taps_side)
    input_grad = back_rest(place, pre_back, mid, edge_near, edge_across, taps_side)
    return (section_out[None], input_grad[None], value_grad.T)


def solution(mesh):
    in_specs = (
        P("groups", "seq", "wide"),
        P(None, "wide", None),
        P(),
        P(),
        P(None, "wide"),
        P(None, "wide"),
        P(None, "wide"),
        P("wide", None),
        P("groups", "seq", None),
    )
    out_specs = (P("groups", "seq", None), P("groups", "seq", "wide"), P(("groups", "wide"), "seq"))
    return jax.shard_map(
        on_device, mesh=mesh, in_specs=in_specs, out_specs=out_specs, check_vma=False
    )
```

```python
import functools
import math

import jax
import jax.numpy as jnp
from jax import lax
from jax.experimental import pallas as pl
from jax.experimental.pallas import tpu as pltpu
from jax.sharding import PartitionSpec as P

DH = 192
EPSILON = 1e-06
SCORE_GAIN = 3.0
GELU_ROOT = 0.7978845608028654
GELU_CUBIC = 0.044715
F32 = jnp.float32
BF16 = jnp.bfloat16
HALO_ROWS = 16
CHUNK = 16
SMEM = pl.BlockSpec(memory_space=pltpu.SMEM)
MIB = 1024 * 1024


def spec():
    return pl.BlockSpec(memory_space=pltpu.VMEM)


def in_hbm():
    return pl.BlockSpec(memory_space=pltpu.HBM)


def anywhere():
    return pl.BlockSpec(memory_space=pl.ANY)


def far(value):
    return pltpu.with_memory_space_constraint(value, pltpu.HBM)


def near_core(value):
    return pltpu.with_memory_space_constraint(value, pltpu.VMEM)


def params(limit=8):
    return pltpu.CompilerParams(vmem_limit_bytes=limit * MIB)


def cost(flops, nbytes):
    return pl.CostEstimate(flops=int(flops), bytes_accessed=int(nbytes), transcendentals=0)


def dot(left, right):
    return jnp.dot(left, right, preferred_element_type=F32)


def dot_rt(left, right):
    return lax.dot_general(left, right, (((1,), (1,)), ((), ())), preferred_element_type=F32)


def dot_lt(left, right):
    return lax.dot_general(left, right, (((0,), (0,)), ((), ())), preferred_element_type=F32)


def pick(shape, test):
    row = lax.broadcasted_iota(jnp.int32, shape, 0)
    col = lax.broadcasted_iota(jnp.int32, shape, 1)
    return jnp.where(test(row, col), 1.0, 0.0).astype(BF16)


def edges_kernel(fine_any, edge_ref, top, low, sems):
    rows = fine_any.shape[0]
    copies = [
        pltpu.make_async_copy(fine_any.at[pl.ds(0, CHUNK)], top, sems.at[0]),
        pltpu.make_async_copy(fine_any.at[pl.ds(rows - CHUNK, CHUNK)], low, sems.at[1]),
    ]
    for c in copies:
        c.start()
    for c in copies:
        c.wait()
    edge_ref[0:2, :] = low[CHUNK - 2 :, :]
    edge_ref[2:3, :] = top[0:1, :]


def edges(fine):
    channels = fine.shape[1]
    return pl.pallas_call(
        edges_kernel,
        out_shape=jax.ShapeDtypeStruct((3, channels), BF16),
        in_specs=[in_hbm()],
        out_specs=spec(),
        scratch_shapes=[
            pltpu.VMEM((CHUNK, channels), BF16),
            pltpu.VMEM((CHUNK, channels), BF16),
            pltpu.SemaphoreType.DMA((2,)),
        ],
        compiler_params=params(),
        cost_estimate=cost(channels, 64 * channels),
        name="edges",
    )(far(fine))


def sided(place_ref, first_ref, second_ref, before_rows):
    even = place_ref[0] % 2 == 0
    first, second = first_ref[...].astype(F32), second_ref[...].astype(F32)
    low = lax.broadcasted_iota(jnp.int32, first.shape, 0) < before_rows
    return jnp.where(low == even, second, first).astype(BF16)


def early_kernel(cot_any, wo_any, grad_ref, cot, wo, sems):
    copies = [
        pltpu.make_async_copy(cot_any, cot, sems.at[0]),
        pltpu.make_async_copy(wo_any, wo, sems.at[1]),
    ]
    for c in copies:
        c.start()
    for c in copies:
        c.wait()
    grad_ref[...] = dot_rt(cot[...], wo[...]).astype(BF16)


def early(cot, wo):
    tok, features = cot.shape
    width = wo.shape[0]
    return pl.pallas_call(
        early_kernel,
        out_shape=jax.ShapeDtypeStruct((tok, width), BF16),
        in_specs=[in_hbm()] * 2,
        out_specs=spec(),
        scratch_shapes=[
            pltpu.VMEM((tok, features), BF16),
            pltpu.VMEM(wo.shape, BF16),
            pltpu.SemaphoreType.DMA((2,)),
        ],
        compiler_params=params(),
        cost_estimate=cost(2 * tok * features * width, 2 * wo.size),
        name="early",
    )(far(cot), far(wo))


def conv_kernel(order, fine_any, taps_any, out_ref, fine, taps, sems):
    fine_rows, channels = fine.shape
    fine_copy = pltpu.make_async_copy(fine_any, fine, sems.at[len(order)])
    fine_copy.start()
    tok = fine_rows // 2
    copies = {k: pltpu.make_async_copy(taps_any.at[k], taps.at[k], sems.at[k]) for k in order}
    for k in order:
        copies[k].start()
    fine_copy.wait()
    block = fine[...]
    total = None
    for k in order:
        rows = dot(pick((tok, fine_rows), lambda r, c, k=k: c == 2 * r + k - 2), block).astype(BF16)
        copies[k].wait()
        term = dot(rows, taps[k])
        total = term if total is None else total + term
    out_ref[...] = total


def conv_inner(fine, weight):
    taps, channels, features = weight.shape
    tok = fine.shape[0] // 2
    return pl.pallas_call(
        functools.partial(conv_kernel, tuple(range(taps))),
        out_shape=jax.ShapeDtypeStruct((tok, features), F32),
        in_specs=[in_hbm()] * 2,
        out_specs=spec(),
        scratch_shapes=[
            pltpu.VMEM(fine.shape, BF16),
            pltpu.VMEM(weight.shape, BF16),
            pltpu.SemaphoreType.DMA((taps + 1,)),
        ],
        compiler_params=params(12),
        cost_estimate=cost(2 * tok * weight.size, 2 * weight.size),
        name="conv_inner",
    )(far(fine), far(weight))


def conv_edge_kernel(place_ref, inner_ref, first_ref, second_ref, taps_any, out_ref, taps, sems):
    tok = inner_ref.shape[0]
    copies = [pltpu.make_async_copy(taps_any.at[k], taps.at[i], sems.at[i]) for i, k in enumerate((0, 1, 4))]
    for c in copies:
        c.start()
    side = sided(place_ref, first_ref, second_ref, 2)
    blank = jnp.zeros((CHUNK - 1, side.shape[1]), BF16)
    terms = []
    for i in range(3):
        copies[i].wait()
        terms.append(dot(jnp.concatenate([side[i : i + 1], blank], 0), taps[i])[0:1])
    row = lax.broadcasted_iota(jnp.int32, (CHUNK, 1), 0)
    top = inner_ref[:CHUNK, :] + jnp.where(row == 0, terms[0] + terms[1], 0.0)
    low = inner_ref[tok - CHUNK :, :] + jnp.where(row == CHUNK - 1, terms[2], 0.0)
    out_ref[:CHUNK, :] = top.astype(BF16)
    out_ref[CHUNK : tok - CHUNK, :] = inner_ref[CHUNK : tok - CHUNK, :].astype(BF16)
    out_ref[tok - CHUNK :, :] = low.astype(BF16)


def conv_edge(place, inner, first, second, weight):
    taps, channels, features = weight.shape
    return pl.pallas_call(
        conv_edge_kernel,
        out_shape=jax.ShapeDtypeStruct(inner.shape, BF16),
        in_specs=[SMEM] + [spec()] * 3 + [in_hbm()],
        out_specs=spec(),
        scratch_shapes=[pltpu.VMEM((3, channels, features), BF16), pltpu.SemaphoreType.DMA((3,))],
        compiler_params=params(8),
        cost_estimate=cost(96 * channels * features, 6 * channels * features),
        name="conv_edge",
    )(place, inner, first, second, far(weight))


def gelu_value(preact):
    tangent = jnp.tanh(GELU_ROOT * (preact + GELU_CUBIC * preact * preact * preact))
    return 0.5 * preact * (1.0 + tangent), tangent


def head_scale(value):
    lane = lax.broadcasted_iota(jnp.int32, value.shape, 1)
    square = value * value
    parts = value.shape[1] // DH
    scale = jnp.zeros_like(value)
    for h in range(parts):
        here = (lane >= h * DH) & (lane < (h + 1) * DH)
        mean = jnp.sum(jnp.where(here, square, 0.0), -1, keepdims=True) * (1.0 / DH)
        scale = jnp.where(here, lax.rsqrt(mean + EPSILON), scale)
    return scale


def head_mean(value):
    lane = lax.broadcasted_iota(jnp.int32, value.shape, 1)
    parts = value.shape[1] // DH
    out = jnp.zeros_like(value)
    for h in range(parts):
        here = (lane >= h * DH) & (lane < (h + 1) * DH)
        mean = jnp.sum(jnp.where(here, value, 0.0), -1, keepdims=True) * (1.0 / DH)
        out = jnp.where(here, mean, out)
    return out


def norm_kernel(wide_ref, mine_ref, theirs_ref, bias_ref, gain_ref, *refs):
    weights_any, (grad_ref, normed_ref, message_ref), weights, sems = refs[:3], refs[3:6], refs[6:9], refs[9]
    tok, features = mine_ref.shape
    width = message_ref.shape[1]
    half = tok // 2
    copies = [pltpu.make_async_copy(weights_any[i], weights[i], sems.at[i]) for i in range(3)]
    for c in copies:
        c.start()

    @pl.loop(0, tok // CHUNK)
    def _(i):
        at = pl.ds(pl.multiple_of(i * CHUNK, CHUNK), CHUNK)
        preact = mine_ref[at, :].astype(F32) + theirs_ref[at, :].astype(F32) + bias_ref[...]
        hidden = gelu_value(preact)[0].astype(BF16).astype(F32)
        inv = lax.rsqrt(jnp.mean(hidden * hidden, -1, keepdims=True) + EPSILON)
        normed_ref[at, :] = (hidden * inv * gain_ref[...]).astype(BF16)

    own = normed_ref[pl.ds(pl.multiple_of(wide_ref[0] * half, CHUNK), half), :]
    for j in range(features // width):
        message_ref[j * half : (j + 1) * half, :] = own[:, j * width : (j + 1) * width]
    message_ref[features // width * half :, :] = grad_ref[...]
    for c in copies:
        c.wait()


def norm(wide, mine, theirs, bias, gain, weights, grad):
    tok, features = mine.shape
    width = weights[0].shape[1]
    rows = features // width * (tok // 2) + tok
    return pl.pallas_call(
        norm_kernel,
        out_shape=[
            jax.ShapeDtypeStruct((tok, features), BF16),
            jax.ShapeDtypeStruct((rows, width), BF16),
        ]
        + [pltpu.VMEM(w.shape, BF16) for w in weights],
        in_specs=[SMEM] + [spec()] * 4 + [in_hbm()] * 3 + [spec()],
        out_specs=[spec()] * 5,
        scratch_shapes=[pltpu.SemaphoreType.DMA((3,))],
        compiler_params=params(),
        cost_estimate=cost(30 * tok * features, 6 * tok * features),
        name="norm",
    )(wide, mine, theirs, bias, gain, *[far(w) for w in weights], grad)


def project(value, chosen, weights, qkv_ref, slice_ref, proj_ref=None):
    width = weights[0].shape[1]
    slice_ref[...] = dot(value, chosen).astype(BF16)
    for i, w in enumerate(weights):
        proj = dot(value, w[...])
        if proj_ref is not None and i < 2:
            proj_ref[:, i * width : (i + 1) * width] = proj
        if i < 2:
            proj = proj * head_scale(proj)
        qkv_ref[:, i * width : (i + 1) * width] = proj.astype(BF16)


def own_kernel(place_ref, normed_ref, grad_ref, wq_ref, wk_ref, wv_ref, qkv_ref, slice_ref, proj_ref, chosen_ref):
    count = slice_ref.shape[1]
    start = place_ref[0] * count
    chosen_ref[...] = pick(chosen_ref.shape, lambda r, c: r == c + start)
    qkv_ref[:, 3 * wq_ref.shape[1] :] = grad_ref[...]
    project(normed_ref[...], chosen_ref[...], (wq_ref, wk_ref, wv_ref), qkv_ref, slice_ref, proj_ref)


def own_project(place, normed, grad, wq, wk, wv, count):
    rows, features = normed.shape
    width = wq.shape[1]
    return pl.pallas_call(
        own_kernel,
        out_shape=[
            jax.ShapeDtypeStruct((rows, 4 * width), BF16),
            jax.ShapeDtypeStruct((rows, count), BF16),
            jax.ShapeDtypeStruct((rows, 2 * width), F32),
            jax.ShapeDtypeStruct((features, count), BF16),
        ],
        in_specs=[SMEM] + [spec()] * 5,
        out_specs=[spec()] * 4,
        compiler_params=params(),
        cost_estimate=cost(6 * rows * features * width, 6 * features * width),
        name="own_project",
    )(place, normed, grad, wq, wk, wv)


def others_kernel(count, half, wide_ref, chosen_ref, *refs):
    mine, theirs = refs[:count], refs[count : 2 * count]
    wq_ref, wk_ref, wv_ref, qkv_ref, slice_ref, lhs = refs[2 * count :]
    width = wq_ref.shape[1]
    for b in range(count):
        for ref, core in ((mine[b], wide_ref[0]), (theirs[b], 1 - wide_ref[0])):
            row = pl.ds(pl.multiple_of(b * 2 * half + core * half, CHUNK), half)
            for j in range(wq_ref.shape[0] // width):
                lhs[row, j * width : (j + 1) * width] = ref[j * half : (j + 1) * half, :]
        base = b * 2 * half
        qkv_ref[base : base + 2 * half, 3 * width :] = mine[b][mine[b].shape[0] - 2 * half :, :]
    project(lhs[...], chosen_ref[...], (wq_ref, wk_ref, wv_ref), qkv_ref, slice_ref)


def others_project(wide, chosen, mine, theirs, wq, wk, wv, count, half):
    features, width = wq.shape
    rows = len(mine) * 2 * half
    return pl.pallas_call(
        functools.partial(others_kernel, len(mine), half),
        out_shape=[
            jax.ShapeDtypeStruct((rows, 4 * width), BF16),
            jax.ShapeDtypeStruct((rows, count), BF16),
        ],
        in_specs=[SMEM] + [spec()] * (2 * len(mine) + 4),
        out_specs=[spec()] * 2,
        scratch_shapes=[pltpu.VMEM((rows, features), BF16)],
        compiler_params=params(),
        cost_estimate=cost(6 * rows * features * width, 6 * features * width),
        name="others_project",
    )(wide, chosen, *mine, *theirs, wq, wk, wv)


def attention_kernel(tok, tile, heads, qkv_rows, *refs):
    groups = len(qkv_rows)
    width = heads * DH
    total = sum(qkv_rows)
    qkv_in = refs[:groups]
    proj_ref, wq, wk, wv, wo, both_ref, dv_ref = refs[groups : groups + 7]
    qkv, dv_acc, dk_acc, dq_acc, att, sems = refs[groups + 7 :]
    at, loads = 0, []
    for i, rows in enumerate(qkv_rows):
        if total <= 1024:
            qkv[at : at + rows, :] = qkv_in[i][...]
        else:
            loads.append(pltpu.make_async_copy(qkv_in[i], qkv.at[pl.ds(at, rows)], sems.at[i]))
        at += rows
    for c in loads:
        c.start()
    for c in loads:
        c.wait()

    scale = SCORE_GAIN / math.sqrt(DH)
    lanes = min(128, tile)

    def block(start, first, h):
        here = pl.ds(start, tile)
        cols = slice(h * DH, (h + 1) * DH)
        key = qkv[:, width + h * DH : width + (h + 1) * DH]
        val = qkv[:, 2 * width + h * DH : 2 * width + (h + 1) * DH]
        query = qkv[here, cols]
        up = qkv[here, 3 * width + h * DH : 3 * width + (h + 1) * DH]
        expo = jnp.exp2(dot_rt(key, query) * (scale * math.log2(math.e)))
        back = dot_rt(val, up)
        inv = 1.0 / jnp.sum(expo, 0, keepdims=True)
        delta = jnp.sum(expo * back, 0, keepdims=True) * inv
        prob_b = (expo * inv).astype(BF16)
        scaled = inv * scale
        score_own = (expo[:tok] * scaled * (back[:tok] - delta)).astype(BF16)
        if tile == total:
            dv_ref[:, cols] = dot(prob_b, up).astype(BF16)
            dk_acc[:, cols] = dot(score_own, query)
        elif first:
            dv_acc[:, cols] = dot(prob_b, up)
            dk_acc[:, cols] = dot(score_own, query)
        else:
            dv_acc[:, cols] += dot(prob_b, up)
            dk_acc[:, cols] += dot(score_own, query)

        def own():
            att[:, cols] = dot_lt(prob_b[:, :lanes], val)[:tok].astype(BF16)
            score = expo[:, :lanes] * scaled[:, :lanes] * (back[:, :lanes] - delta[:, :lanes])
            dq_acc[:, cols] = dot_lt(score.astype(BF16), key)[:tok]

        if first:
            own()
        elif first is None:
            pl.when(start == 0)(own)

    if total <= 1024:
        for step in range(total // tile):
            for h in range(heads):
                block(step * tile, step == 0, h)
    else:
        dv_acc[...] = jnp.zeros_like(dv_acc)
        dk_acc[...] = jnp.zeros_like(dk_acc)
        for h in range(heads):

            @pl.loop(0, total // tile)
            def _(step):
                block(pl.multiple_of(step * tile, tile), None, h)

    if tile != total:
        dv_ref[...] = dv_acc[...].astype(BF16)
    both_ref[:tok, :] = dot(att[...], wo[...]).astype(BF16)
    backs = []
    for acc, lo in ((dq_acc, 0), (dk_acc, width)):
        proj = proj_ref[:, lo : lo + width]
        inv = head_scale(proj)
        normal = proj * inv
        up = acc[...].astype(BF16).astype(F32)
        backs.append((inv * (up - normal * head_mean(up * normal))).astype(BF16))
    norm_back = dot_rt(backs[0], wq[...]) + dot_rt(backs[1], wk[...]) + dot_rt(dv_ref[:tok, :], wv[...])
    both_ref[tok:, :] = norm_back.astype(BF16)


def attention(qkvs, proj, wq, wk, wv, wo, tok):
    qkv_rows = tuple(a.shape[0] for a in qkvs)
    total = sum(qkv_rows)
    features, width = wq.shape
    heads = width // DH
    tile = total if total <= 1024 else 128
    return pl.pallas_call(
        functools.partial(attention_kernel, tok, tile, heads, qkv_rows),
        out_shape=[
            jax.ShapeDtypeStruct((2 * tok, features), BF16),
            jax.ShapeDtypeStruct((total, width), BF16),
        ],
        in_specs=[spec() if total <= 1024 else anywhere()] * len(qkvs) + [spec()] * 5,
        out_specs=[spec()] * 2,
        scratch_shapes=[
            pltpu.VMEM((total, 4 * width), BF16),
            pltpu.VMEM((total, width), F32),
            pltpu.VMEM((tok, width), F32),
            pltpu.VMEM((tok, width), F32),
            pltpu.VMEM((tok, width), BF16),
            pltpu.SemaphoreType.DMA((len(qkvs),)),
        ],
        compiler_params=params(32 if total <= 1024 else 56),
        cost_estimate=cost(6 * total * total * width, 8 * total * width),
        name="attention",
    )(*qkvs, proj, wq, wk, wv, wo)


def local_kernel(mine_ref, theirs_ref, bias_ref, hidden_ref, slope_ref):
    @pl.loop(0, mine_ref.shape[0] // CHUNK)
    def _(i):
        at = pl.ds(pl.multiple_of(i * CHUNK, CHUNK), CHUNK)
        preact = mine_ref[at, :].astype(F32) + theirs_ref[at, :].astype(F32) + bias_ref[...]
        active, tangent = gelu_value(preact)
        hidden_ref[at, :] = active.astype(BF16)
        slope_ref[at, :] = 0.5 * (1.0 + tangent) + 0.5 * preact * (1.0 - tangent * tangent) * GELU_ROOT * (
            1.0 + 3.0 * GELU_CUBIC * preact * preact
        )


def local_terms(mine, theirs, bias):
    return pl.pallas_call(
        local_kernel,
        out_shape=[jax.ShapeDtypeStruct(mine.shape, BF16), jax.ShapeDtypeStruct(mine.shape, F32)],
        in_specs=[spec()] * 3,
        out_specs=[spec()] * 2,
        compiler_params=params(),
        cost_estimate=cost(40 * mine.size, 10 * mine.size),
        name="local_terms",
    )(mine, theirs, bias)


def finish_kernel(hidden_ref, slope_ref, gain_ref, cot_ref, here_ref, there_ref, *refs):
    taps_any, out_ref, pre_ref, edge_ref, taps_ref, sem = refs
    tok = out_ref.shape[0]
    copy = pltpu.make_async_copy(taps_any.at[pl.ds(2, 2)], taps_ref, sem)
    copy.start()

    @pl.loop(0, tok // CHUNK)
    def _(i):
        at = pl.ds(pl.multiple_of(i * CHUNK, CHUNK), CHUNK)
        low = pl.ds(pl.multiple_of(tok + i * CHUNK, CHUNK), CHUNK)
        hidden = hidden_ref[at, :].astype(F32)
        inv = lax.rsqrt(jnp.mean(hidden * hidden, -1, keepdims=True) + EPSILON)
        out_ref[at, :] = (hidden + (here_ref[at, :].astype(F32) + there_ref[at, :].astype(F32))).astype(BF16)
        gain_back = (here_ref[low, :].astype(F32) + there_ref[low, :].astype(F32)) * gain_ref[...]
        mean = jnp.mean(gain_back * hidden, -1, keepdims=True)
        back = cot_ref[at, :].astype(F32) + inv * (gain_back - hidden * (inv * inv * mean))
        pre_ref[at, :] = (back * slope_ref[at, :]).astype(BF16)

    edge_ref[0:1, :] = pre_ref[tok - 1 : tok, :]
    edge_ref[1:2, :] = pre_ref[0:1, :]
    copy.wait()


def finish(hidden, slope, gain, cot, here, there, taps):
    tok, features = cot.shape
    row = jax.ShapeDtypeStruct((2, features), BF16)
    full = jax.ShapeDtypeStruct((tok, features), BF16)
    return pl.pallas_call(
        finish_kernel,
        out_shape=[full, full, row, pltpu.VMEM((2,) + taps.shape[1:], BF16)],
        in_specs=[spec()] * 6 + [in_hbm()],
        out_specs=[spec()] * 4,
        scratch_shapes=[pltpu.SemaphoreType.DMA],
        compiler_params=params(16),
        cost_estimate=cost(40 * tok * features, 12 * tok * features),
        name="finish",
    )(hidden, slope, gain, cot, here, there, far(taps))


def back_mid_kernel(pre_ref, weight_ref, taps_any, out_ref, taps_ref, sems):
    channels = weight_ref.shape[1]
    copies = [pltpu.make_async_copy(taps_any.at[k], taps_ref.at[i], sems.at[i]) for i, k in enumerate((0, 1, 4))]
    for c in copies:
        c.start()
    pre = pre_ref[...]
    out_ref[:, :channels] = dot_rt(pre, weight_ref[0])
    out_ref[:, channels:] = dot_rt(pre, weight_ref[1])
    for c in copies:
        c.wait()


def back_mid(pre, weight, taps):
    tok, features = pre.shape
    channels = weight.shape[1]
    return pl.pallas_call(
        back_mid_kernel,
        out_shape=[
            jax.ShapeDtypeStruct((tok, 2 * channels), F32),
            pltpu.VMEM((3,) + taps.shape[1:], BF16),
        ],
        in_specs=[spec()] * 2 + [in_hbm()],
        out_specs=[spec()] * 2,
        scratch_shapes=[pltpu.SemaphoreType.DMA((3,))],
        compiler_params=params(),
        cost_estimate=cost(4 * tok * channels * features, 10 * channels * features),
        name="back_mid",
    )(pre, weight, far(taps))


def back_rest_kernel(place_ref, pre_ref, mid_ref, first_ref, second_ref, weight_ref, out_ref):
    tok, channels = pre_ref.shape[0], weight_ref.shape[1]
    pre = pre_ref[...]
    side = sided(place_ref, first_ref, second_ref, 1)
    after = jnp.concatenate([pre[1:], side[1:2]], 0)
    before = jnp.concatenate([side[0:1], pre[:-1]], 0)
    first = mid_ref[:, :channels] + dot_rt(after, weight_ref[0]) + dot_rt(before, weight_ref[2])
    second = mid_ref[:, channels:] + dot_rt(after, weight_ref[1])
    even = pick((2 * tok, tok), lambda r, c: r == 2 * c)
    odd = pick((2 * tok, tok), lambda r, c: r == 2 * c + 1)
    out_ref[...] = (dot(even, first.astype(BF16)) + dot(odd, second.astype(BF16))).astype(BF16)


def back_rest(place, pre, mid, first, second, weight):
    tok, features = pre.shape
    channels = weight.shape[1]
    return pl.pallas_call(
        back_rest_kernel,
        out_shape=jax.ShapeDtypeStruct((2 * tok, channels), BF16),
        in_specs=[SMEM] + [spec()] * 5,
        out_specs=spec(),
        compiler_params=params(),
        cost_estimate=cost(6 * tok * channels * features, 6 * channels * features),
        name="back_rest",
    )(place, pre, mid, first, second, weight)


def value_kernel(rows_of, scale, dv_ref, *refs):
    slices, out_ref = refs[:-1], refs[-1]
    total, at = None, 0
    for ref, rows in zip(slices, rows_of):
        term = dot_lt(ref[...], dv_ref[at : at + rows, :])
        total = term if total is None else total + term
        at += rows
    out_ref[...] = total * scale


def value_gradient(dv, slices, scale):
    rows_of = tuple(a.shape[0] for a in slices)
    return pl.pallas_call(
        functools.partial(value_kernel, rows_of, scale),
        out_shape=jax.ShapeDtypeStruct((slices[0].shape[1], dv.shape[1]), F32),
        in_specs=[spec()] * (1 + len(slices)),
        out_specs=spec(),
        compiler_params=params(),
        cost_estimate=cost(2 * dv.shape[0] * dv.shape[1] * 192, 2 * dv.size),
        name="value_gradient",
    )(dv, *slices)


def on_device(
    fine_input,
    conv_weight,
    conv_bias,
    norm_gain,
    query_weight,
    key_weight,
    value_weight,
    out_weight,
    cotangent,
):
    samples, fine_rows, channels = fine_input.shape
    tok = fine_rows // 2
    taps, _, features = conv_weight.shape
    n = lax.axis_size("seq")
    grad_scale = 1.0 / math.sqrt(samples * tok * n)
    near = [(i, i ^ 1) for i in range(n)]
    across = [(i, i + 1) for i in range(1, n - 1, 2)] + [(i + 1, i) for i in range(1, n - 1, 2)]
    cycle = list(range(0, n, 2)) + list(range(n - 1, 0, -2))
    ahead = [(cycle[i], cycle[(i + 1) % n]) for i in range(n)]
    behind = [(j, i) for i, j in ahead]
    swap = [(0, 1), (1, 0)]
    place = lax.axis_index("seq").astype(jnp.int32).reshape(1)
    wide = lax.axis_index("wide").astype(jnp.int32).reshape(1)
    bias, gain = conv_bias.reshape(1, features), norm_gain.reshape(1, features)
    fine, cot = fine_input[0], cotangent[0]
    count, core_rows = features // n, tok // 2
    weights = (query_weight, key_weight, value_weight)

    edge = edges(fine)
    edge_near, edge_across = lax.ppermute(edge, "seq", near), lax.ppermute(edge, "seq", across)
    att_grad = early(cot, out_weight)
    inner = conv_inner(fine, conv_weight)
    mine = conv_edge(place, inner, edge_near, edge_across, conv_weight)
    theirs = lax.ppermute(mine, "wide", swap)
    normed, message, *weights = norm(wide, mine, theirs, bias, gain, weights, att_grad)
    weights = [near_core(w) for w in weights]

    local = local_terms(mine, theirs, bias)
    qkvs, slices = [], []
    cw = ccw = message
    ready = proj = None
    for k in range(1, n // 2 + 1):
        if k == 2:
            cw, ccw, qkvs[0] = lax.optimization_barrier((cw, ccw, qkvs[0]))
        elif k == 3:
            cw, ccw, local = lax.optimization_barrier((cw, ccw, local))
        elif k > 3:
            cw, ccw, qkvs[k - 3], qkvs[k - 2] = lax.optimization_barrier(
                (cw, ccw, qkvs[k - 3], qkvs[k - 2])
            )
        if k < n // 2:
            cw, ccw = lax.ppermute(cw, "seq", ahead), lax.ppermute(ccw, "seq", behind)
            blocks = [cw, ccw]
        else:
            blocks = [lax.ppermute(cw, "seq", ahead)]
        sisters = [lax.ppermute(a, "wide", swap) for a in blocks]
        if k == 1:
            qkv, piece, proj, chosen = own_project(place, normed, att_grad, *weights, count)
        else:
            qkv, piece = others_project(wide, chosen, *ready, *weights, count, core_rows)
        qkvs.append(qkv)
        slices.append(piece)
        ready = (blocks, sisters)
    qkv, piece = others_project(wide, chosen, *ready, *weights, count, core_rows)
    qkvs.append(qkv)
    slices.append(piece)

    both, dv = attention(qkvs, proj, *weights, out_weight, tok)
    there = lax.ppermute(both, "wide", swap)
    value_grad = value_gradient(dv, slices, grad_scale)
    section_out, pre_back, edge, taps_here = finish(
        *local, gain, cot, both, there, conv_weight
    )
    edge_near, edge_across = lax.ppermute(edge, "seq", near), lax.ppermute(edge, "seq", across)
    taps_here = near_core(taps_here)
    mid, taps_side = back_mid(pre_back, taps_here, conv_weight)
    taps_side = near_core(taps_side)
    input_grad = back_rest(place, pre_back, mid, edge_near, edge_across, taps_side)
    return (section_out[None], input_grad[None], value_grad.T)


def solution(mesh):
    in_specs = (
        P("groups", "seq", "wide"),
        P(None, "wide", None),
        P(),
        P(),
        P(None, "wide"),
        P(None, "wide"),
        P(None, "wide"),
        P("wide", None),
        P("groups", "seq", None),
    )
    out_specs = (P("groups", "seq", None), P("groups", "seq", "wide"), P(("groups", "wide"), "seq"))
    return jax.shard_map(
        on_device, mesh=mesh, in_specs=in_specs, out_specs=out_specs, check_vma=False
    )
```
